128 devices in a mesh: seed: 4 (over z), tok: 32 (over x, y, core).
Axes of the slice: x: 4, y: 4, z: 4, core: 2. Of those that a mesh axis runs over, the one named last changes fastest.
Arguments:
- atom_single: bfloat16 [32768, 128], P(('seed', 'tok')), parts along dimension 0, may hold values from -6 to 6
- atom_bias: bfloat16 [8192, 512], P('tok'), may hold values from -400 to 400
- atom_token: int32 [8192], P('tok'), may hold values from 0 to 1023, as said below
- atom_counts: int32 [1024], P('tok'), may hold values from 1 to 15, as said below
- pair_rep: bfloat16 [1024, 1024, 128], P('tok'), may hold values from -400 to 400
- atom_qkv_w: bfloat16 [128, 384], replicated, may hold values from -0.5 to 0.5
- atom_out_w: bfloat16 [128, 128], replicated, may hold values from -0.5 to 0.5
- agg_w: bfloat16 [128, 768], replicated, may hold values from -0.5 to 0.5
- tok_qkv_w: bfloat16 [2, 768, 2304], replicated, may hold values from -0.21875 to 0.21875
- tok_out_w: bfloat16 [2, 768, 768], replicated, may hold values from -0.4375 to 0.4375
- pair_w: bfloat16 [128, 32], replicated, may hold values from -0.5 to 0.5
- bcast_w: bfloat16 [768, 128], replicated, may hold values from -0.21875 to 0.21875
Outputs:
- atom_out: bfloat16 [32768, 128], P(('seed', 'tok')), parts along dimension 0
- token_out: bfloat16 [4096, 768], P(('seed', 'tok')), parts along dimension 0
The draws below stay inside these ranges and needn't reach their ends.
There are 4 independent parts, one for each index of `seed`. The reference program is written for one: setup_inputs(seed, part) draws one part's arguments, and reference() takes and returns one part's arrays. A program takes and returns all parts, laid end to end along the dimension named above; an argument that names none is the same for every part. Nothing has to cross between parts.
Inputs may be any that keep to these rules, and one draw needn't show every extreme that they name: `atom_counts`: counts sum to 8192; the counts of the tokens of one index of tok sum to 256; the largest count is 15 and the smallest 1 in every draw. `atom_token`: token t holds exactly atom_counts[t] atoms, and the atoms of one token are consecutive. Along the atoms the tokens come in increasing order, except that at each boundary between neighbouring indices of tok the first token of the upper index comes just before the last token of the lower index; so every atom belongs to a token of its own index of tok or of a neighbouring one.
All inputs are finite; a program needn't handle non-finite values.
Results may differ from the reference program's by a relative error of at most 0.017.
Values may be sent and summed in bfloat16 or wider, within the bound.
No kernel may reach another device: no remote copies, remote signals or barrier semaphores. Data moves between devices by JAX's collectives and lax.ppermute only.
A program may use at most 128 MiB of HBM per device.

```python
import jax
import jax.numpy as jnp
from jax import lax

C = 768
H = 16
CZ = 128
CA = 128
AH = 4
QW = 32
KW = 128
ATOMS_PER_TOKEN = 8
NB = 2
TOK_DEV = 32
TOKENS = 1024
ATOMS = 8192
HALO = 48
N_TOK = 32


def atom_layout(key):
    jitter = jax.random.randint(key, (TOKENS // 2,), -3, 4)
    jitter = jitter.at[0].set(ATOMS_PER_TOKEN - 1)
    counts = jnp.stack([ATOMS_PER_TOKEN + jitter, ATOMS_PER_TOKEN - jitter], axis=1).reshape(TOKENS).astype(jnp.int32)
    lower = jnp.arange(N_TOK - 1, dtype=jnp.int32) * TOK_DEV + TOK_DEV - 1
    upper = lower + 1
    order = jnp.arange(TOKENS, dtype=jnp.int32)
    order = order.at[lower].set(upper).at[upper].set(lower)
    ends = jnp.cumsum(counts[order]).astype(jnp.int32)
    place = jnp.searchsorted(ends, jnp.arange(ATOMS, dtype=jnp.int32), side='right')
    owner = order[place]
    return (counts, owner.astype(jnp.int32))


def draw_atom_counts(key, part):
    counts, owner = atom_layout(key)
    return counts


def draw_atom_token(key, part):
    counts, owner = atom_layout(key)
    return owner


def draw_atom_bias(key, part):
    key = jax.random.fold_in(key, 11)
    key_base = jax.random.fold_in(key, 0)
    base = jnp.clip(jax.random.normal(key_base, (ATOMS, AH * KW), jnp.float32), -6.0, 6.0)
    return base.astype(jnp.bfloat16)


def draw_pair_rep(key, part):
    key = jax.random.fold_in(key, 23)
    key_base = jax.random.fold_in(key, 0)
    base = jnp.clip(jax.random.normal(key_base, (TOKENS, TOKENS, CZ), jnp.float32), -6.0, 6.0)
    return base.astype(jnp.bfloat16)


def levels(key, extent, cuts, least, largest):
    def one(dim, blocks):
        steps = jax.random.uniform(jax.random.fold_in(jax.random.fold_in(key, 6), dim), (blocks,), jnp.float32, least / len(cuts), largest / len(cuts))
        return jnp.repeat(jnp.exp(steps), extent[dim] // blocks).reshape((-1,) + (1,) * (len(extent) - dim - 1))

    level = one(*cuts[0])
    for cut in cuts[1:]:
        level = level * one(*cut)
    return level


def gaussian(stream_key, extent, spread, limit, pieces=(), held_as=jnp.bfloat16):
    entries = spread * jax.random.normal(stream_key, extent, jnp.float32)
    if pieces:
        entries = entries * levels(stream_key, extent, pieces, -0.22, 0.18)
    return jnp.clip(entries, -limit, limit).astype(held_as)


def setup_inputs(seed: int = 0, part: int = 0) -> dict:
    splits = jax.random.split(jax.random.key(seed), 13)
    part_keys = jax.random.split(jax.random.fold_in(splits[12], part), 13)
    return {
        "atom_single": gaussian(part_keys[0], (ATOMS, CA), 1.0, 6.0, ((0, 32),)),
        "atom_bias": draw_atom_bias(jax.random.fold_in(splits[12], 71), part),
        "atom_token": draw_atom_token(jax.random.fold_in(splits[12], 71), part),
        "atom_counts": draw_atom_counts(jax.random.fold_in(splits[12], 71), part),
        "pair_rep": draw_pair_rep(jax.random.fold_in(splits[12], 71), part),
        "atom_qkv_w": gaussian(splits[5], (CA, 3 * CA), CA ** -0.5, 0.5),
        "atom_out_w": gaussian(splits[6], (CA, CA), CA ** -0.5, 0.5),
        "agg_w": gaussian(splits[7], (CA, C), CA ** -0.5, 0.5),
        "tok_qkv_w": gaussian(splits[8], (NB, C, 3 * C), C ** -0.5, 0.21875),
        "tok_out_w": gaussian(splits[9], (NB, C, C), (C // 4) ** -0.5, 0.4375),
        "pair_w": gaussian(splits[10], (CZ, NB * H), CZ ** -0.5, 0.5),
        "bcast_w": gaussian(splits[11], (C, CA), C ** -0.5, 0.21875),
    }


def layer_norm(values):
    average = lax.optimization_barrier(jnp.mean(values, axis=-1, keepdims=True))
    centred = values - average
    variance = lax.optimization_barrier(jnp.mean(centred * centred, axis=-1, keepdims=True))
    return centred * lax.rsqrt(variance + 1e-05)

def window_attend(queries, keyvals, atom_bias, first_atom, atom_total):
    windows = keyvals.shape[0]
    head_width = CA // AH
    query_heads = queries.reshape(windows, QW, AH, head_width).astype(jnp.float32)
    key_heads = keyvals[:, :, :CA].reshape(windows, KW, AH, head_width).astype(jnp.float32)
    value_heads = keyvals[:, :, CA:].reshape(windows, KW, AH, head_width).astype(jnp.float32)
    scores = jnp.einsum('wqhd,wkhd->whqk', query_heads, key_heads) * head_width ** (-0.5)
    scores = scores + atom_bias.reshape(windows, QW, AH, KW).transpose(0, 2, 1, 3).astype(jnp.float32)
    position = first_atom + QW * jnp.arange(windows, dtype=jnp.int32)[:, None] - HALO + jnp.arange(KW, dtype=jnp.int32)[None, :]
    inside = (position >= 0) & (position < atom_total)
    scores = jnp.where(inside[:, None, None, :], scores, -1000000000.0)
    maximum = lax.optimization_barrier(jnp.max(scores, axis=-1, keepdims=True))
    powers = jnp.exp(scores - maximum)
    denominator = lax.optimization_barrier(jnp.sum(powers, axis=-1))
    weights = lax.optimization_barrier(powers.astype(jnp.bfloat16)).astype(jnp.float32)
    mixed_heads = jnp.einsum('whqk,wkhd->wqhd', weights, value_heads) / denominator.transpose(0, 2, 1)[..., None]
    return mixed_heads.reshape(windows * QW, CA).astype(jnp.bfloat16)

def reference(atom_single, atom_bias, atom_token, atom_counts, pair_rep, atom_qkv_w, atom_out_w, agg_w, tok_qkv_w, tok_out_w, pair_w, bcast_w):
    hidden_in = atom_single.astype(jnp.float32)
    normed = layer_norm(hidden_in).astype(jnp.bfloat16)
    projected = jnp.dot(normed, atom_qkv_w, preferred_element_type=jnp.float32).astype(jnp.bfloat16)
    queries = projected[:, :CA]
    padded = jnp.pad(projected[:, CA:], ((HALO, HALO), (0, 0)))
    windows = ATOMS // QW
    gather_index = QW * jnp.arange(windows, dtype=jnp.int32)[:, None] + jnp.arange(KW, dtype=jnp.int32)[None, :]
    keyvals = padded[gather_index]
    attended = window_attend(queries, keyvals, atom_bias, 0, ATOMS)
    atom_hidden = (hidden_in + jnp.dot(attended, atom_out_w, preferred_element_type=jnp.float32)).astype(jnp.bfloat16)
    lifted = jax.nn.relu(jnp.dot(atom_hidden, agg_w, preferred_element_type=jnp.float32))
    token_sums = jax.ops.segment_sum(lifted, atom_token, num_segments=TOKENS)
    stream = token_sums / atom_counts.astype(jnp.float32)[:, None]

    def project_rows(row_block):
        return jnp.einsum('ijc,ch->hij', row_block.astype(jnp.float32), pair_w.astype(jnp.float32)).astype(jnp.bfloat16)
    pair_bias = lax.map(project_rows, pair_rep.reshape(N_TOK, TOK_DEV, TOKENS, CZ))
    pair_bias = pair_bias.transpose(1, 0, 2, 3).reshape(NB * H, TOKENS, TOKENS)
    head_size = C // H

    def one_head(operands):
        query_rows, key_rows, value_rows, bias_rows = operands
        scores = jnp.dot(query_rows, key_rows.T, preferred_element_type=jnp.float32) * head_size ** (-0.5)
        scores = scores + bias_rows.astype(jnp.float32)
        maximum = lax.optimization_barrier(jnp.max(scores, axis=-1, keepdims=True))
        powers = jnp.exp(scores - maximum)
        denominator = lax.optimization_barrier(jnp.sum(powers, axis=-1))
        weights = powers.astype(jnp.bfloat16)
        return jnp.dot(weights, value_rows, preferred_element_type=jnp.float32) / denominator[:, None]
    for layer_index in range(NB):
        normed = layer_norm(stream).astype(jnp.bfloat16)
        projected = jnp.dot(normed, tok_qkv_w[layer_index], preferred_element_type=jnp.float32).astype(jnp.bfloat16)
        query_heads = projected[:, :C].reshape(TOKENS, H, head_size).transpose(1, 0, 2)
        key_heads = projected[:, C:2 * C].reshape(TOKENS, H, head_size).transpose(1, 0, 2)
        value_heads = projected[:, 2 * C:].reshape(TOKENS, H, head_size).transpose(1, 0, 2)
        bias_layer = pair_bias[layer_index * H:(layer_index + 1) * H]
        mixed_heads = lax.map(one_head, (query_heads, key_heads, value_heads, bias_layer))
        mixed_heads = mixed_heads.transpose(1, 0, 2).reshape(TOKENS, C).astype(jnp.bfloat16)
        stream = stream + jnp.dot(mixed_heads, tok_out_w[layer_index], preferred_element_type=jnp.float32)
    token_out = stream.astype(jnp.bfloat16)
    token_carry = jnp.dot(token_out, bcast_w, preferred_element_type=jnp.float32).astype(jnp.bfloat16)
    picked = jnp.take(token_carry, atom_token, axis=0)
    atom_out = (atom_hidden.astype(jnp.float32) + picked.astype(jnp.float32)).astype(jnp.bfloat16)
    return (atom_out, token_out)
```

```python
import functools

import jax
import jax.numpy as jnp
from jax import lax
from jax.experimental import pallas as pl
from jax.experimental.pallas import tpu as pltpu
from jax.sharding import PartitionSpec as P

C = 768
H = 16
HEAD = C // H
CA = 128
AH = 4
QW = 32
KW = 128
HALO = 48
EDGE = 16
REACH = EDGE + 64
TOKD = 32
ATOMD = 256
ROWS = 48
QROWS = 34 * H
KEYS = 1024
HALF = 512
CHUNK = 32
PACK = REACH + 4 * EDGE + 16
F32 = jnp.float32
BF16 = jnp.bfloat16

NT = (((1,), (1,)), ((), ()))


def params(mib):
    return pltpu.CompilerParams(vmem_limit_bytes=mib * 1024 * 1024)


VMEM = pl.BlockSpec(memory_space=pltpu.VMEM)


def layer_norm(values):
    average = jnp.mean(values, axis=-1, keepdims=True)
    centred = values - average
    variance = jnp.mean(centred * centred, axis=-1, keepdims=True)
    return centred * lax.rsqrt(variance + 1e-05)


def chunk_starts(tok):
    core, y, x = lax.rem(tok, 2), lax.rem(tok // 2, 4), tok // 8
    starts = []
    for j in range(32):
        slow, fast = (j % 16) // 4, j % 4
        plane = core if j < 16 else 1 - core
        kx = jnp.where(plane == 0, slow, fast)
        ky = jnp.where(plane == 0, fast, slow)
        starts.append((((x ^ kx) * 4 + (y ^ ky)) * 2 + plane) * CHUNK)
    return starts


def ordered(pair_ref, t, starts):
    return jnp.concatenate(
        [pair_ref[t, pl.ds(pl.multiple_of(s, CHUNK), CHUNK), :] for s in starts], axis=0
    )


def pack_kernel(single_ref, low_bias_ref, high_bias_ref, token_ref, low_pair_ref, high_pair_ref,
                pair_w_ref, down_ref, up_ref, down_bias_ref, up_bias_ref):
    tok = lax.axis_index("tok")
    base = tok * TOKD
    for out_ref, bias_ref, rows, lanes in (
        (down_ref, low_bias_ref, slice(0, REACH), slice(0, 128)),
        (up_ref, high_bias_ref, slice(ATOMD - REACH, ATOMD), slice(128, 256)),
    ):
        out_ref[:REACH] = single_ref[rows, :]
        for h in range(AH):
            out_ref[REACH + EDGE * h : REACH + EDGE * (h + 1)] = bias_ref[:, h * KW : (h + 1) * KW]
        relative = (token_ref[:, lanes] - base).astype(F32)
        out_ref[REACH + AH * EDGE :] = jnp.broadcast_to(relative, (16, 128)).astype(BF16)
    weights = pair_w_ref[...]
    for out_ref, pair_ref, owner in (
        (down_bias_ref, low_pair_ref, jnp.maximum(tok - 1, 0)),
        (up_bias_ref, high_pair_ref, jnp.minimum(tok + 1, 31)),
    ):
        rows = ordered(pair_ref, 0, chunk_starts(owner))
        out_ref[...] = lax.dot_general(weights, rows, NT, preferred_element_type=F32).astype(BF16)


STEP = 4


def bias_kernel(pair_ref, pair_w_ref, bias0_ref, bias1_ref):
    starts = chunk_starts(lax.axis_index("tok"))
    weights = pair_w_ref[...]
    for t in range(STEP):
        rows = ordered(pair_ref, t, starts)
        out = lax.dot_general(weights, rows, NT, preferred_element_type=F32).astype(BF16)
        bias0_ref[t * H : (t + 1) * H] = out[:H]
        bias1_ref[t * H : (t + 1) * H] = out[H:]


def atom_kernel(single_ref, lower_ref, upper_ref, bias_ref, token_ref, qkv_ref, out_w_ref, agg_ref,
                hidden_ref, stream_ref, normed_ref, own_ref, proj_ref, mixed_ref):
    tok = lax.axis_index("tok")
    first_atom = tok * ATOMD
    base = tok * TOKD
    everything = jnp.concatenate(
        [lower_ref[:REACH], single_ref[...], upper_ref[:REACH]], axis=0
    ).astype(F32)
    normed = layer_norm(everything).astype(BF16)
    proj_ref[...] = jnp.dot(normed, qkv_ref[...], preferred_element_type=F32).astype(BF16)
    head_of_lane = lax.broadcasted_iota(jnp.int32, (1, CA), 1) // (CA // AH)
    windows = [(REACH + QW * w, QW, 32 + QW * w, QW * w) for w in range(8)]
    windows += [(REACH + ATOMD, EDGE, 288, ATOMD), (REACH - EDGE, EDGE, 0, 384 - EDGE)]
    mixed_ref[ATOMD + EDGE : 384 - EDGE] = jnp.zeros((384 - 2 * EDGE - ATOMD, CA), BF16)
    for q_row, count, k_row, out_row in windows:
        queries = proj_ref[q_row : q_row + count, :CA]
        keys = proj_ref[k_row : k_row + KW, CA : 2 * CA]
        values = proj_ref[k_row : k_row + KW, 2 * CA :]
        stacked = jnp.concatenate(
            [jnp.where(head_of_lane == h, queries, jnp.zeros_like(queries)) for h in range(AH)], axis=0
        )
        if out_row < ATOMD:
            bias = [bias_ref[out_row : out_row + count, h * KW : (h + 1) * KW] for h in range(AH)]
        else:
            ref = upper_ref if out_row == ATOMD else lower_ref
            bias = [ref[REACH + EDGE * h : REACH + EDGE * (h + 1)] for h in range(AH)]
        scores = lax.dot_general(stacked, keys, NT, preferred_element_type=F32) * (CA // AH) ** (-0.5)
        scores = scores + jnp.concatenate(bias, axis=0).astype(F32)
        position = (
            first_atom + (k_row - REACH) + lax.broadcasted_iota(jnp.int32, (1, KW), 1)
        )
        inside = (position >= 0) & (position < 32 * ATOMD)
        scores = jnp.where(inside, scores, -1000000000.0)
        powers = jnp.exp(scores - jnp.max(scores, axis=-1, keepdims=True))
        total = jnp.sum(powers, axis=-1, keepdims=True)
        mixed = jnp.dot(powers.astype(BF16), values, preferred_element_type=F32) / total
        merged = jnp.where(head_of_lane == 0, mixed[:count], 0.0)
        for h in range(1, AH):
            merged = jnp.where(head_of_lane == h, mixed[h * count : (h + 1) * count], merged)
        mixed_ref[out_row : out_row + count] = merged.astype(BF16)
    hidden_in = jnp.concatenate(
        [
            single_ref[...],
            upper_ref[:EDGE],
            jnp.zeros((384 - 2 * EDGE - ATOMD, CA), BF16),
            lower_ref[REACH - EDGE : REACH],
        ],
        axis=0,
    ).astype(F32)
    hidden = (
        hidden_in + jnp.dot(mixed_ref[...], out_w_ref[...], preferred_element_type=F32)
    ).astype(BF16)
    hidden_ref[...] = hidden[:ATOMD]
    lifted = jnp.maximum(jnp.dot(hidden, agg_ref[...], preferred_element_type=F32), 0.0)
    lane = lax.broadcasted_iota(jnp.int32, (1, 128), 1)
    after = upper_ref[REACH + AH * EDGE :][:1].astype(F32).astype(jnp.int32) + TOKD
    before = lower_ref[REACH + AH * EDGE :][:1].astype(F32).astype(jnp.int32) - TOKD
    near = jnp.where(lane < EDGE, after, jnp.where(lane >= 128 - EDGE, before, -100))
    relative = jnp.concatenate([token_ref[...] - base, near], axis=1)
    row = lax.broadcasted_iota(jnp.int32, (ROWS, 1), 0)
    wanted = jnp.where(row < TOKD, row, jnp.where(row == TOKD, -1, jnp.where(row == TOKD + 1, TOKD, -200)))
    member = (relative == wanted).astype(F32)
    counts = jnp.maximum(jnp.sum(member, axis=-1, keepdims=True), 1.0)
    picker = member.astype(BF16)
    upper = lifted.astype(BF16)
    lower = (lifted - upper.astype(F32)).astype(BF16)
    sums = jnp.dot(picker, upper, preferred_element_type=F32)
    sums = sums + jnp.dot(picker, lower, preferred_element_type=F32)
    stream = sums / counts
    stream_ref[...] = stream
    out = layer_norm(stream).astype(BF16)
    normed_ref[...] = out
    own_ref[...] = out[:TOKD]


def head_mask():
    row = lax.broadcasted_iota(jnp.int32, (QROWS, 1), 0)
    lane = lax.broadcasted_iota(jnp.int32, (1, C), 1)
    start = (row & (H - 1)) * HEAD
    return (lane >= start) & (lane < start + HEAD)


def query_kernel(normed_ref, q_ref, k_ref, out_ref):
    queries = jnp.dot(normed_ref[...], q_ref[...], preferred_element_type=F32).astype(BF16)
    row = lax.broadcasted_iota(jnp.int32, (QROWS, ROWS), 0)
    column = lax.broadcasted_iota(jnp.int32, (QROWS, ROWS), 1)
    spread = ((row >> 4) == column).astype(F32).astype(BF16)
    repeated = jnp.dot(spread, queries, preferred_element_type=F32)
    repeated = jnp.where(head_mask(), repeated, 0.0).astype(BF16)
    lifted = lax.dot_general(repeated, k_ref[...], NT, preferred_element_type=F32)
    out_ref[...] = (lifted * HEAD ** (-0.5)).astype(BF16)


def attend(query_ref, near_ref, far_ref, bias_ref, edge_bias_ref, v_ref, out_w_ref, stream_ref):
    queries = query_ref[...]
    halves = []
    for i, ref in enumerate((near_ref, far_ref)):
        scores = lax.dot_general(queries, ref[...], NT, preferred_element_type=F32)
        bias = jnp.concatenate(
            [bias_ref[:, i * HALF : (i + 1) * HALF], edge_bias_ref[:, i * HALF : (i + 1) * HALF]], axis=0
        )
        halves.append(scores + bias.astype(F32))
    maximum = jnp.maximum(
        jnp.max(halves[0], axis=-1, keepdims=True), jnp.max(halves[1], axis=-1, keepdims=True)
    )
    total = 0.0
    mixed = 0.0
    for scores, ref in zip(halves, (near_ref, far_ref)):
        powers = jnp.exp(scores - maximum)
        total = total + jnp.sum(powers, axis=-1, keepdims=True)
        mixed = mixed + jnp.dot(powers.astype(BF16), ref[...], preferred_element_type=F32)
    mixed = (mixed / total).astype(BF16)
    valued = jnp.dot(mixed, v_ref[...], preferred_element_type=F32)
    valued = jnp.where(head_mask(), valued, 0.0).astype(BF16)
    row = lax.broadcasted_iota(jnp.int32, (ROWS, QROWS), 0)
    column = lax.broadcasted_iota(jnp.int32, (ROWS, QROWS), 1)
    gather = ((column >> 4) == row).astype(F32).astype(BF16)
    heads = jnp.dot(gather, valued, preferred_element_type=F32).astype(BF16)
    return stream_ref[...] + jnp.dot(heads, out_w_ref[...], preferred_element_type=F32)


def middle_kernel(*refs):
    stream_ref, normed_ref, own_ref = refs[8:]
    stream = attend(*refs[:8])
    stream_ref[...] = stream
    out = layer_norm(stream).astype(BF16)
    normed_ref[...] = out
    own_ref[...] = out[:TOKD]


def last_kernel(*refs):
    bcast_ref, token_ref, hidden_ref, atom_out_ref, token_out_ref = refs[8:]
    token_out = attend(*refs[:8]).astype(BF16)
    token_out_ref[...] = token_out[:TOKD]
    carry = jnp.dot(token_out, bcast_ref[...], preferred_element_type=F32).astype(BF16)
    relative = token_ref[...] - lax.axis_index("tok") * TOKD
    row = lax.broadcasted_iota(jnp.int32, (ROWS, 1), 0)
    wanted = jnp.where(row < TOKD, row, jnp.where(row == TOKD, -1, jnp.where(row == TOKD + 1, TOKD, -200)))
    member = (relative == wanted).astype(F32).astype(BF16)
    picked = lax.dot_general(member, carry, (((0,), (0,)), ((), ())), preferred_element_type=F32)
    atom_out_ref[...] = (hidden_ref[...].astype(F32) + picked).astype(BF16)


def flips(dx, dy, dc):
    pairs = []
    for tok in range(32):
        core, y, x = tok % 2, (tok // 2) % 4, tok // 8
        pairs.append((tok, ((x ^ dx) * 4 + (y ^ dy)) * 2 + (core ^ dc)))
    return pairs


def crossed(k, first):
    along_y, along_x = flips(0, k, 0), flips(k, 0, 0)
    return [
        (along_y if (tok % 2 == 0) == first else along_x)[tok] for tok in range(32)
    ]


def gather(own):
    for first in (True, False):
        own = jnp.concatenate(
            [own] + [lax.ppermute(own, "tok", crossed(k, first)) for k in (1, 2, 3)], axis=0
        )
    return own, lax.ppermute(own, "tok", flips(0, 0, 1))


def shape(rows, columns, dtype=BF16):
    return jax.ShapeDtypeStruct((rows, columns), dtype)


def local(atom_single, atom_bias, atom_token, atom_counts, pair_rep, atom_qkv_w, atom_out_w, agg_w,
          tok_qkv_w, tok_out_w, pair_w, bcast_w):
    tokens = atom_token.reshape(1, ATOMD)
    pair_wt = pair_w.T
    down = [(i + 1, i) for i in range(31)]
    up = [(i, i + 1) for i in range(31)]

    to_down, to_up, bias_down, bias_up = pl.pallas_call(
        pack_kernel,
        grid=(1,),
        in_specs=[
            pl.BlockSpec((ATOMD, CA), lambda i: (0, 0)),
            pl.BlockSpec((EDGE, AH * KW), lambda i: (0, 0)),
            pl.BlockSpec((EDGE, AH * KW), lambda i: (ATOMD // EDGE - 1, 0)),
            pl.BlockSpec((1, ATOMD), lambda i: (0, 0)),
            pl.BlockSpec((1, KEYS, 128), lambda i: (0, 0, 0)),
            pl.BlockSpec((1, KEYS, 128), lambda i: (TOKD - 1, 0, 0)),
            pl.BlockSpec((32, 128), lambda i: (0, 0)),
        ],
        out_specs=[pl.BlockSpec((PACK, CA), lambda i: (0, 0))] * 2 + [pl.BlockSpec((32, KEYS), lambda i: (0, 0))] * 2,
        out_shape=[shape(PACK, CA)] * 2 + [shape(32, KEYS)] * 2,
        compiler_params=params(8),
        name="pack",
    )(atom_single, atom_bias, atom_bias, tokens, pair_rep, pair_rep, pair_wt)
    from_upper = lax.ppermute(to_down, "tok", down)
    from_lower = lax.ppermute(to_up, "tok", up)
    upper_bias = lax.ppermute(bias_down, "tok", down)
    lower_bias = lax.ppermute(bias_up, "tok", up)

    bias = pl.pallas_call(
        bias_kernel,
        grid=(TOKD // STEP,),
        in_specs=[
            pl.BlockSpec((STEP, KEYS, 128), lambda i: (i, 0, 0)),
            pl.BlockSpec((32, 128), lambda i: (0, 0)),
        ],
        out_specs=[pl.BlockSpec((STEP * H, KEYS), lambda i: (i, 0))] * 2,
        out_shape=[shape(TOKD * H, KEYS)] * 2,
        compiler_params=params(12),
        cost_estimate=pl.CostEstimate(flops=2 * 32 * 1024 * 128 * 32, bytes_accessed=10 * 2**20, transcendentals=0),
        name="bias",
    )(pair_rep, pair_wt)
    edge_bias = [
        jnp.concatenate([lower_bias[b * H : (b + 1) * H], upper_bias[b * H : (b + 1) * H]], axis=0)
        for b in range(2)
    ]

    hidden, stream, normed, own = pl.pallas_call(
        atom_kernel,
        in_specs=[VMEM] * 8,
        out_specs=[VMEM] * 4,
        out_shape=[shape(ATOMD, CA), shape(ROWS, C, F32), shape(ROWS, C), shape(TOKD, C)],
        scratch_shapes=[pltpu.VMEM((2 * REACH + ATOMD, 3 * CA), BF16), pltpu.VMEM((384, CA), BF16)],
        compiler_params=params(16),
        name="atoms",
    )(atom_single, from_lower, from_upper, atom_bias, tokens, atom_qkv_w, atom_out_w, agg_w)

    for layer in range(2):
        near, far = gather(own)
        queries = pl.pallas_call(
            query_kernel,
            grid=(1,),
            in_specs=[
                pl.BlockSpec((ROWS, C), lambda i: (0, 0)),
                pl.BlockSpec((None, C, C), lambda i, layer=layer: (layer, 0, 0)),
                pl.BlockSpec((None, C, C), lambda i, layer=layer: (layer, 0, 1)),
            ],
            out_specs=pl.BlockSpec((QROWS, C), lambda i: (0, 0)),
            out_shape=shape(QROWS, C),
            compiler_params=params(20),
            cost_estimate=pl.CostEstimate(flops=10**9, bytes_accessed=5 * 2**20, transcendentals=0),
            name="queries",
        )(normed, tok_qkv_w, tok_qkv_w)
        whole = lambda rows, columns: pl.BlockSpec((rows, columns), lambda i: (0, 0))
        in_specs = [
            whole(QROWS, C),
            whole(HALF, C),
            whole(HALF, C),
            whole(TOKD * H, KEYS),
            whole(2 * H, KEYS),
            pl.BlockSpec((None, C, C), lambda i, layer=layer: (layer, 0, 2)),
            pl.BlockSpec((None, C, C), lambda i, layer=layer: (layer, 0, 0)),
            whole(ROWS, C),
        ]
        operands = (queries, near, far, bias[layer], edge_bias[layer], tok_qkv_w, tok_out_w, stream)
        if layer == 0:
            stream, normed, own = pl.pallas_call(
                middle_kernel,
                grid=(1,),
                in_specs=in_specs,
                out_specs=[whole(ROWS, C), whole(ROWS, C), whole(TOKD, C)],
                out_shape=[shape(ROWS, C, F32), shape(ROWS, C), shape(TOKD, C)],
                compiler_params=params(32),
                name="block",
            )(*operands)
        else:
            atom_out, token_out = pl.pallas_call(
                last_kernel,
                grid=(1,),
                in_specs=in_specs + [whole(C, CA), whole(1, ATOMD), whole(ATOMD, CA)],
                out_specs=[whole(ATOMD, CA), whole(TOKD, C)],
                out_shape=[shape(ATOMD, CA), shape(TOKD, C)],
                compiler_params=params(32),
                name="block_and_broadcast",
            )(*operands, bcast_w, tokens, hidden)
    return (atom_out, token_out)


def solution(mesh):
    placed = (
        P(("seed", "tok"), None),
        P("tok", None),
        P("tok"),
        P("tok"),
        P("tok", None, None),
        P(),
        P(),
        P(),
        P(),
        P(),
        P(),
        P(),
    )
    return jax.shard_map(
        local,
        mesh=mesh,
        in_specs=placed,
        out_specs=(P(("seed", "tok"), None), P(("seed", "tok"), None)),
        check_vma=False,
    )
```

```python
import functools

import jax
import jax.numpy as jnp
from jax import lax
from jax.experimental import pallas as pl
from jax.experimental.pallas import tpu as pltpu
from jax.sharding import PartitionSpec as P

C = 768
H = 16
HEAD = C // H
CA = 128
AH = 4
QW = 32
KW = 128
HALO = 48
EDGE = 16
REACH = EDGE + 64
TOKD = 32
ATOMD = 256
ROWS = 48
QROWS = 34 * H
KEYS = 1024
HALF = 512
CHUNK = 32
INFO = REACH + AH * EDGE
PAIR = INFO + 16
PACK = PAIR + 8 * 32
F32 = jnp.float32
BF16 = jnp.bfloat16

NT = (((1,), (1,)), ((), ()))


def params(mib):
    return pltpu.CompilerParams(vmem_limit_bytes=mib * 1024 * 1024)


VMEM = pl.BlockSpec(memory_space=pltpu.VMEM)


def layer_norm(values):
    average = jnp.mean(values, axis=-1, keepdims=True)
    centred = values - average
    variance = jnp.mean(centred * centred, axis=-1, keepdims=True)
    return centred * lax.rsqrt(variance + 1e-05)


def chunk_starts(tok):
    core, y, x = lax.rem(tok, 2), lax.rem(tok // 2, 4), tok // 8
    starts = []
    for j in range(32):
        slow, fast = (j % 16) // 4, j % 4
        plane = core if j < 16 else 1 - core
        kx = jnp.where(plane == 0, slow, fast)
        ky = jnp.where(plane == 0, fast, slow)
        starts.append((((x ^ kx) * 4 + (y ^ ky)) * 2 + plane) * CHUNK)
    return starts


def ordered(pair_ref, t, starts):
    return jnp.concatenate(
        [pair_ref[t, pl.ds(pl.multiple_of(s, CHUNK), CHUNK), :] for s in starts], axis=0
    )


def pack_kernel(single_hbm, bias_hbm, token_hbm, pair_hbm, pair_w_hbm, down_ref, up_ref,
                single_ref, edge_ref, token_ref, pair_ref, pair_w_ref, sems):
    copies = [
        pltpu.make_async_copy(pair_hbm.at[0], pair_ref.at[0], sems.at[0]),
        pltpu.make_async_copy(pair_hbm.at[TOKD - 1], pair_ref.at[1], sems.at[1]),
        pltpu.make_async_copy(pair_w_hbm, pair_w_ref, sems.at[2]),
        pltpu.make_async_copy(single_hbm.at[pl.ds(0, REACH)], single_ref.at[0], sems.at[3]),
        pltpu.make_async_copy(single_hbm.at[pl.ds(ATOMD - REACH, REACH)], single_ref.at[1], sems.at[4]),
        pltpu.make_async_copy(bias_hbm.at[pl.ds(0, EDGE)], edge_ref.at[0], sems.at[5]),
        pltpu.make_async_copy(bias_hbm.at[pl.ds(ATOMD - EDGE, EDGE)], edge_ref.at[1], sems.at[6]),
        pltpu.make_async_copy(token_hbm, token_ref, sems.at[7]),
    ]
    for copy in copies:
        copy.start()
    tok = lax.axis_index("tok")
    base = tok * TOKD
    orders = [chunk_starts(jnp.maximum(tok - 1, 0)), chunk_starts(jnp.minimum(tok + 1, 31))]
    for copy in copies[3:]:
        copy.wait()
    for side, out_ref in enumerate((down_ref, up_ref)):
        out_ref[:REACH] = single_ref[side]
        for h in range(AH):
            out_ref[REACH + EDGE * h : REACH + EDGE * (h + 1)] = edge_ref[side, :, h * KW : (h + 1) * KW]
        relative = (token_ref[:, side * 128 : (side + 1) * 128] - base).astype(F32)
        out_ref[INFO : INFO + 16] = jnp.broadcast_to(relative, (16, 128)).astype(BF16)
    copies[2].wait()
    weights = pair_w_ref[...]
    for side, out_ref in enumerate((down_ref, up_ref)):
        copies[side].wait()
        rows = ordered(pair_ref, side, orders[side])
        out = lax.dot_general(weights, rows, NT, preferred_element_type=F32).astype(BF16)
        for k in range(8):
            out_ref[PAIR + 32 * k : PAIR + 32 * (k + 1)] = out[:, 128 * k : 128 * (k + 1)]


def bias_kernel(pair_ref, pair_w_ref, bias0_ref, bias1_ref):
    starts = chunk_starts(lax.axis_index("tok"))
    weights = pair_w_ref[...]
    for t in range(TOKD):
        rows = ordered(pair_ref, t, starts)
        out = lax.dot_general(weights, rows, NT, preferred_element_type=F32).astype(BF16)
        bias0_ref[t * H : (t + 1) * H] = out[:H]
        bias1_ref[t * H : (t + 1) * H] = out[H:]


def windowed(proj_ref, k_row, q_row, count, bias, first_atom):
    head_of_lane = lax.broadcasted_iota(jnp.int32, (1, CA), 1) // (CA // AH)
    queries = proj_ref[q_row : q_row + count, :CA]
    keys = proj_ref[k_row : k_row + KW, CA : 2 * CA]
    values = proj_ref[k_row : k_row + KW, 2 * CA :]
    stacked = jnp.concatenate(
        [jnp.where(head_of_lane == h, queries, jnp.zeros_like(queries)) for h in range(AH)], axis=0
    )
    scores = lax.dot_general(stacked, keys, NT, preferred_element_type=F32) * (CA // AH) ** (-0.5)
    scores = scores + jnp.concatenate(bias, axis=0).astype(F32)
    position = first_atom + k_row + lax.broadcasted_iota(jnp.int32, (1, KW), 1)
    inside = (position >= 0) & (position < 32 * ATOMD)
    scores = jnp.where(inside, scores, -1000000000.0)
    powers = jnp.exp(scores - jnp.max(scores, axis=-1, keepdims=True))
    total = jnp.sum(powers, axis=-1, keepdims=True)
    mixed = jnp.dot(powers.astype(BF16), values, preferred_element_type=F32) / total
    merged = jnp.where(head_of_lane == 0, mixed[:count], 0.0)
    for h in range(1, AH):
        merged = jnp.where(head_of_lane == h, mixed[h * count : (h + 1) * count], merged)
    return merged.astype(BF16)


def projected(rows, qkv_ref):
    normed = layer_norm(rows.astype(F32)).astype(BF16)
    return jnp.dot(normed, qkv_ref[...], preferred_element_type=F32).astype(BF16)


def own_bias(bias_ref, w):
    return [bias_ref[QW * w : QW * (w + 1), h * KW : (h + 1) * KW] for h in range(AH)]


def wanted_tokens():
    row = lax.broadcasted_iota(jnp.int32, (ROWS, 1), 0)
    return jnp.where(row < TOKD, row, jnp.where(row == TOKD, -1, jnp.where(row == TOKD + 1, TOKD, -200)))


def hidden_and_sums(hidden_in, mixed, relative, out_w_ref, agg_ref):
    hidden = (
        hidden_in.astype(F32) + jnp.dot(mixed, out_w_ref[...], preferred_element_type=F32)
    ).astype(BF16)
    lifted = jnp.maximum(jnp.dot(hidden, agg_ref[...], preferred_element_type=F32), 0.0)
    member = (relative == wanted_tokens()).astype(F32)
    counts = jnp.sum(member, axis=-1, keepdims=True)
    picker = member.astype(BF16)
    upper = lifted.astype(BF16)
    lower = (lifted - upper.astype(F32)).astype(BF16)
    sums = jnp.dot(picker, upper, preferred_element_type=F32)
    sums = sums + jnp.dot(picker, lower, preferred_element_type=F32)
    return hidden, sums, counts


def inner_atom_kernel(*refs):
    sources, refs = refs[:6], refs[6:]
    single_ref, bias_ref, token_ref, qkv_ref, out_w_ref, agg_ref = refs[:6]
    proj_ref, hidden_ref, sums_ref, counts_ref, mixed_ref, sems = refs[6:]
    copies = [
        pltpu.make_async_copy(source, ref, sems.at[i]) for i, (source, ref) in enumerate(zip(sources, refs))
    ]
    for copy in copies:
        copy.start()
    tok = lax.axis_index("tok")
    for copy in copies:
        copy.wait()
    proj_ref[...] = projected(single_ref[...], qkv_ref)
    for i, w in enumerate((4, 5, 2, 3)):
        mixed_ref[QW * i : QW * (i + 1)] = windowed(
            proj_ref, QW * w - HALO, QW * w, QW, own_bias(bias_ref, w), tok * ATOMD
        )
    lane = lax.broadcasted_iota(jnp.int32, (1, 128), 1)
    relative = jnp.where(lane < 64, token_ref[:, 128:], token_ref[:, :128]) - tok * TOKD
    hidden_in = jnp.concatenate([single_ref[128:192], single_ref[64:128]], axis=0)
    hidden, sums, counts = hidden_and_sums(hidden_in, mixed_ref[...], relative, out_w_ref, agg_ref)
    hidden_ref[:64] = hidden[64:]
    hidden_ref[64:] = hidden[:64]
    sums_ref[...] = sums
    counts_ref[...] = jnp.broadcast_to(counts, counts_ref.shape)


def atom_kernel(single_ref, lower_ref, upper_ref, bias_ref, token_ref, qkv_ref, out_w_ref, agg_ref,
                inner_ref, inner_hidden_ref, inner_sums_ref, inner_counts_ref,
                hidden_ref, stream_ref, normed_ref, own_ref, edge0_ref, edge1_ref, proj_ref, mixed_ref):
    tok = lax.axis_index("tok")
    first_atom = tok * ATOMD - REACH
    beside = projected(jnp.concatenate([lower_ref[:REACH], upper_ref[:REACH]], axis=0), qkv_ref)
    proj_ref[:REACH] = beside[:REACH]
    proj_ref[REACH : REACH + ATOMD] = inner_ref[...]
    proj_ref[REACH + ATOMD :] = beside[REACH:]
    mixed_ref[128 + EDGE : 256 - EDGE] = jnp.zeros((128 - 2 * EDGE, CA), BF16)
    for i, w in enumerate((0, 1, 6, 7)):
        mixed_ref[QW * i : QW * (i + 1)] = windowed(
            proj_ref, 32 + QW * w, REACH + QW * w, QW, own_bias(bias_ref, w), first_atom
        )
    for out_row, q_row, k_row, ref in (
        (128, REACH + ATOMD, 288, upper_ref), (256 - EDGE, REACH - EDGE, 0, lower_ref)
    ):
        bias = [ref[REACH + EDGE * h : REACH + EDGE * (h + 1)] for h in range(AH)]
        mixed_ref[out_row : out_row + EDGE] = windowed(proj_ref, k_row, q_row, EDGE, bias, first_atom)
    hidden_in = jnp.concatenate(
        [
            single_ref[:64],
            single_ref[192:],
            upper_ref[:EDGE],
            jnp.zeros((128 - 2 * EDGE, CA), BF16),
            lower_ref[REACH - EDGE : REACH],
        ],
        axis=0,
    )
    lane = lax.broadcasted_iota(jnp.int32, (1, 128), 1)
    after = upper_ref[INFO : INFO + 16][:1].astype(F32).astype(jnp.int32) + TOKD
    before = lower_ref[INFO : INFO + 16][:1].astype(F32).astype(jnp.int32) - TOKD
    near = jnp.where(lane < EDGE, after, jnp.where(lane >= 128 - EDGE, before, -100))
    outer = jnp.where(lane < 64, token_ref[:, :128], token_ref[:, 128:]) - tok * TOKD
    hidden, sums, counts = hidden_and_sums(
        hidden_in, mixed_ref[...], jnp.concatenate([outer, near], axis=1), out_w_ref, agg_ref
    )
    hidden_ref[:64] = hidden[:64]
    hidden_ref[64:192] = inner_hidden_ref[...]
    hidden_ref[192:] = hidden[64:128]
    stream = (sums + inner_sums_ref[...]) / jnp.maximum(counts + inner_counts_ref[:, :1], 1.0)
    stream_ref[...] = stream
    out = layer_norm(stream).astype(BF16)
    normed_ref[...] = out
    own_ref[...] = out[:TOKD]
    for block, ref in enumerate((edge0_ref, edge1_ref)):
        for side, source in enumerate((lower_ref, upper_ref)):
            for k in range(8):
                first = PAIR + 32 * k + H * block
                ref[H * side : H * (side + 1), 128 * k : 128 * (k + 1)] = source[first : first + H]


def head_mask():
    row = lax.broadcasted_iota(jnp.int32, (QROWS, 1), 0)
    lane = lax.broadcasted_iota(jnp.int32, (1, C), 1)
    start = (row & (H - 1)) * HEAD
    return (lane >= start) & (lane < start + HEAD)


def query_kernel(layer, normed_ref, qkv_ref, out_ref):
    queries = jnp.dot(normed_ref[...], qkv_ref[layer, :, :C], preferred_element_type=F32).astype(BF16)
    row = lax.broadcasted_iota(jnp.int32, (QROWS, ROWS), 0)
    column = lax.broadcasted_iota(jnp.int32, (QROWS, ROWS), 1)
    spread = ((row >> 4) == column).astype(F32).astype(BF16)
    repeated = jnp.dot(spread, queries, preferred_element_type=F32)
    repeated = jnp.where(head_mask(), repeated, 0.0).astype(BF16)
    lifted = lax.dot_general(repeated, qkv_ref[layer, :, C : 2 * C], NT, preferred_element_type=F32)
    out_ref[...] = (lifted * HEAD ** (-0.5)).astype(BF16)


def join_kernel(count, *refs):
    out_ref = refs[-1]
    rows = out_ref.shape[0] // 4
    for i, place in enumerate((0, 1, 3, 2)):
        out_ref[place * rows : (place + 1) * rows] = refs[i][...]


def scored(query_ref, rows_ref, bias_ref, edge_bias_ref, half):
    lanes = slice(half * HALF, (half + 1) * HALF)
    scores = lax.dot_general(query_ref[...], rows_ref[...], NT, preferred_element_type=F32)
    return scores + jnp.concatenate([bias_ref[:, lanes], edge_bias_ref[:, lanes]], axis=0).astype(F32)


def near_kernel(query_ref, near_ref, bias_ref, edge_bias_ref, mixed_ref, maximum_ref, total_ref):
    scores = scored(query_ref, near_ref, bias_ref, edge_bias_ref, 0)
    maximum = jnp.max(scores, axis=-1, keepdims=True)
    powers = jnp.exp(scores - maximum)
    maximum_ref[...] = jnp.broadcast_to(maximum, maximum_ref.shape)
    total_ref[...] = jnp.broadcast_to(jnp.sum(powers, axis=-1, keepdims=True), total_ref.shape)
    mixed_ref[...] = jnp.dot(powers.astype(BF16), near_ref[...], preferred_element_type=F32)


def attend(layer, query_ref, far_ref, bias_ref, edge_bias_ref, mixed_ref, maximum_ref, total_ref,
           qkv_ref, out_w_ref, stream_ref):
    scores = scored(query_ref, far_ref, bias_ref, edge_bias_ref, 1)
    near_maximum = maximum_ref[:, :1]
    maximum = jnp.maximum(near_maximum, jnp.max(scores, axis=-1, keepdims=True))
    powers = jnp.exp(scores - maximum)
    fade = jnp.exp(near_maximum - maximum)
    total = total_ref[:, :1] * fade + jnp.sum(powers, axis=-1, keepdims=True)
    mixed = mixed_ref[...] * fade + jnp.dot(powers.astype(BF16), far_ref[...], preferred_element_type=F32)
    mixed = (mixed / total).astype(BF16)
    valued = jnp.dot(mixed, qkv_ref[layer, :, 2 * C :], preferred_element_type=F32)
    valued = jnp.where(head_mask(), valued, 0.0).astype(BF16)
    row = lax.broadcasted_iota(jnp.int32, (ROWS, QROWS), 0)
    column = lax.broadcasted_iota(jnp.int32, (ROWS, QROWS), 1)
    gather = ((column >> 4) == row).astype(F32).astype(BF16)
    heads = jnp.dot(gather, valued, preferred_element_type=F32).astype(BF16)
    return stream_ref[...] + jnp.dot(heads, out_w_ref[layer], preferred_element_type=F32)


def middle_kernel(*refs):
    stream_ref, normed_ref, own_ref = refs[10:]
    stream = attend(0, *refs[:10])
    stream_ref[...] = stream
    out = layer_norm(stream).astype(BF16)
    normed_ref[...] = out
    own_ref[...] = out[:TOKD]


def last_kernel(*refs):
    bcast_ref, token_ref, hidden_ref, atom_out_ref, token_out_ref = refs[10:]
    token_out = attend(1, *refs[:10]).astype(BF16)
    token_out_ref[...] = token_out[:TOKD]
    carry = jnp.dot(token_out, bcast_ref[...], preferred_element_type=F32).astype(BF16)
    relative = token_ref[...] - lax.axis_index("tok") * TOKD
    member = (relative == wanted_tokens()).astype(F32).astype(BF16)
    picked = lax.dot_general(member, carry, (((0,), (0,)), ((), ())), preferred_element_type=F32)
    atom_out_ref[...] = (hidden_ref[...].astype(F32) + picked).astype(BF16)


def flips(dx, dy, dc):
    pairs = []
    for tok in range(32):
        core, y, x = tok % 2, (tok // 2) % 4, tok // 8
        pairs.append((tok, ((x ^ dx) * 4 + (y ^ dy)) * 2 + (core ^ dc)))
    return pairs


def crossed(k, first):
    along_y, along_x = flips(0, k, 0), flips(k, 0, 0)
    return [
        (along_y if (tok % 2 == 0) == first else along_x)[tok] for tok in range(32)
    ]


def join(pieces, after):
    return pl.pallas_call(
        functools.partial(join_kernel, len(after)),
        in_specs=[VMEM] * 4 + [pl.BlockSpec(memory_space=pl.ANY)] * len(after),
        out_specs=VMEM,
        out_shape=shape(4 * pieces[0].shape[0], C),
        compiler_params=params(4),
        name="join",
    )(*pieces, *after)


def exchange(rows, first):
    return [rows] + [lax.ppermute(rows, "tok", crossed(k, first)) for k in (1, 3, 2)]


def in_hbm(*arrays):
    return [pltpu.with_memory_space_constraint(x, pltpu.HBM) for x in arrays]


def shape(rows, columns, dtype=BF16):
    return jax.ShapeDtypeStruct((rows, columns), dtype)


def local(atom_single, atom_bias, atom_token, atom_counts, pair_rep, atom_qkv_w, atom_out_w, agg_w,
          tok_qkv_w, tok_out_w, pair_w, bcast_w):
    tokens = atom_token.reshape(1, ATOMD)
    pair_wt = pair_w.T
    hbm = pl.BlockSpec(memory_space=pltpu.HBM)

    to_down, to_up = pl.pallas_call(
        pack_kernel,
        in_specs=[hbm] * 5,
        out_specs=[VMEM] * 2,
        out_shape=[shape(PACK, CA)] * 2,
        scratch_shapes=[
            pltpu.VMEM((2, REACH, CA), BF16),
            pltpu.VMEM((2, EDGE, AH * KW), BF16),
            pltpu.VMEM((1, ATOMD), jnp.int32),
            pltpu.VMEM((2, KEYS, 128), BF16),
            pltpu.VMEM((32, 128), BF16),
            pltpu.SemaphoreType.DMA((8,)),
        ],
        compiler_params=params(8),
        name="pack",
    )(*in_hbm(atom_single, atom_bias, tokens, pair_rep, pair_wt))
    from_upper = lax.ppermute(to_down, "tok", [((i + 1) % 32, i) for i in range(32)])
    from_lower = lax.ppermute(to_up, "tok", [(i, (i + 1) % 32) for i in range(32)])

    bias = pl.pallas_call(
        bias_kernel,
        in_specs=[VMEM] * 2,
        out_specs=[VMEM] * 2,
        out_shape=[shape(TOKD * H, KEYS)] * 2,
        compiler_params=params(12),
        cost_estimate=pl.CostEstimate(flops=2 * 32 * 1024 * 128 * 32, bytes_accessed=10 * 2**20, transcendentals=0),
        name="bias",
    )(pair_rep, pair_wt)

    small = (atom_single, atom_bias, tokens, atom_qkv_w, atom_out_w, agg_w)
    inner = pl.pallas_call(
        inner_atom_kernel,
        in_specs=[hbm] * 6,
        out_specs=[VMEM] * 10,
        out_shape=[jax.ShapeDtypeStruct(x.shape, x.dtype) for x in small]
        + [
            shape(ATOMD, 3 * CA),
            shape(4 * QW, CA),
            shape(ROWS, C, F32),
            shape(ROWS, 128, F32),
        ],
        scratch_shapes=[pltpu.VMEM((4 * QW, CA), BF16), pltpu.SemaphoreType.DMA((6,))],
        compiler_params=params(8),
        cost_estimate=pl.CostEstimate(flops=10**9, bytes_accessed=5 * 2**20, transcendentals=0),
        name="inner_atoms",
    )(*in_hbm(*small))
    single, *rest = inner
    hidden, stream, normed, own, *edge_bias = pl.pallas_call(
        atom_kernel,
        in_specs=[VMEM] * 12,
        out_specs=[VMEM] * 6,
        out_shape=[shape(ATOMD, CA), shape(ROWS, C, F32), shape(ROWS, C), shape(TOKD, C)] + [shape(2 * H, KEYS)] * 2,
        scratch_shapes=[pltpu.VMEM((2 * REACH + ATOMD, 3 * CA), BF16), pltpu.VMEM((256, CA), BF16)],
        compiler_params=params(8),
        name="atoms",
    )(single, from_lower, from_upper, *rest)

    for layer in range(2):
        pieces = exchange(own, True)
        queries = pl.pallas_call(
            functools.partial(query_kernel, layer),
            in_specs=[VMEM] * 2,
            out_specs=VMEM,
            out_shape=shape(QROWS, C),
            compiler_params=params(16),
            cost_estimate=pl.CostEstimate(flops=10**9, bytes_accessed=5 * 2**20, transcendentals=0),
            name="queries",
        )(normed, tok_qkv_w)
        pieces = exchange(join(pieces, [queries]), False)
        near = join(pieces, [bias[0]] if layer == 0 else [])
        far = lax.ppermute(near, "tok", flips(0, 0, 1))
        partial = pl.pallas_call(
            near_kernel,
            in_specs=[VMEM] * 4,
            out_specs=[VMEM] * 3,
            out_shape=[shape(QROWS, C, F32)] + [shape(QROWS, 128, F32)] * 2,
            compiler_params=params(16),
            cost_estimate=pl.CostEstimate(flops=2 * 10**9, bytes_accessed=5 * 2**20, transcendentals=300000),
            name="near",
        )(queries, near, bias[layer], edge_bias[layer])
        operands = (queries, far, bias[layer], edge_bias[layer], *partial, tok_qkv_w, tok_out_w, stream)
        if layer == 0:
            stream, normed, own = pl.pallas_call(
                middle_kernel,
                in_specs=[VMEM] * 10,
                out_specs=[VMEM] * 3,
                out_shape=[shape(ROWS, C, F32), shape(ROWS, C), shape(TOKD, C)],
                compiler_params=params(16),
                name="block",
            )(*operands)
        else:
            atom_out, token_out = pl.pallas_call(
                last_kernel,
                in_specs=[VMEM] * 13,
                out_specs=[VMEM] * 2,
                out_shape=[shape(ATOMD, CA), shape(TOKD, C)],
                compiler_params=params(16),
                name="block_and_broadcast",
            )(*operands, bcast_w, rest[1], hidden)
    return (atom_out, token_out)


def solution(mesh):
    placed = (
        P(("seed", "tok"), None),
        P("tok", None),
        P("tok"),
        P("tok"),
        P("tok", None, None),
        P(),
        P(),
        P(),
        P(),
        P(),
        P(),
        P(),
    )
    return jax.shard_map(
        local,
        mesh=mesh,
        in_specs=placed,
        out_specs=(P(("seed", "tok"), None), P(("seed", "tok"), None)),
        check_vma=False,
    )
```

```python
import functools

import jax
import jax.numpy as jnp
from jax import lax
from jax.experimental import pallas as pl
from jax.experimental.pallas import tpu as pltpu
from jax.sharding import PartitionSpec as P

C = 768
H = 16
HEAD = C // H
CA = 128
AH = 4
QW = 32
KW = 128
HALO = 48
EDGE = 16
REACH = EDGE + 64
TOKD = 32
ATOMD = 256
ROWS = 48
QROWS = 34 * H
KEYS = 1024
HALF = 512
CHUNK = 32
INFO = REACH + AH * EDGE
PAIR = INFO + 16
PACK = PAIR + 8 * 32
F32 = jnp.float32
BF16 = jnp.bfloat16

NT = (((1,), (1,)), ((), ()))


def params(mib):
    return pltpu.CompilerParams(vmem_limit_bytes=mib * 1024 * 1024)


VMEM = pl.BlockSpec(memory_space=pltpu.VMEM)


def layer_norm(values):
    average = jnp.mean(values, axis=-1, keepdims=True)
    centred = values - average
    variance = jnp.mean(centred * centred, axis=-1, keepdims=True)
    return centred * lax.rsqrt(variance + 1e-05)


def chunk_starts(tok):
    core, y, x = lax.rem(tok, 2), lax.rem(tok // 2, 4), tok // 8
    starts = []
    for j in range(32):
        slow, fast = (j % 16) // 4, j % 4
        plane = core if j < 16 else 1 - core
        kx = jnp.where(plane == 0, slow, fast)
        ky = jnp.where(plane == 0, fast, slow)
        starts.append((((x ^ kx) * 4 + (y ^ ky)) * 2 + plane) * CHUNK)
    return starts


def ordered(pair_ref, t, starts):
    return jnp.concatenate(
        [pair_ref[t, pl.ds(pl.multiple_of(s, CHUNK), CHUNK), :] for s in starts], axis=0
    )


def pack_kernel(*refs):
    sources, refs = refs[:8], refs[8:]
    down_ref, up_ref, single_ref, edge_ref, token_ref = refs[:5]
    pair_ref, pair_w_ref, sems = refs[8:]
    pair_hbm, pair_w_hbm = sources[6:]
    copies = [
        pltpu.make_async_copy(source, ref, sems.at[i])
        for i, (source, ref) in enumerate(zip(sources[:3], refs[2:5]))
    ]
    copies += [
        pltpu.make_async_copy(pair_w_hbm, pair_w_ref, sems.at[3]),
        pltpu.make_async_copy(pair_hbm.at[0], pair_ref.at[0], sems.at[4]),
        pltpu.make_async_copy(pair_hbm.at[TOKD - 1], pair_ref.at[1], sems.at[5]),
    ]
    copies += [
        pltpu.make_async_copy(source, ref, sems.at[6 + i])
        for i, (source, ref) in enumerate(zip(sources[3:6], refs[5:8]))
    ]
    for copy in copies:
        copy.start()
    tok = lax.axis_index("tok")
    base = tok * TOKD
    orders = [chunk_starts(jnp.maximum(tok - 1, 0)), chunk_starts(jnp.minimum(tok + 1, 31))]
    for copy in copies[:3]:
        copy.wait()
    for side, out_ref in enumerate((down_ref, up_ref)):
        atoms = slice(0, REACH) if side == 0 else slice(ATOMD - REACH, ATOMD)
        edge = slice(0, EDGE) if side == 0 else slice(ATOMD - EDGE, ATOMD)
        out_ref[:REACH] = single_ref[atoms]
        for h in range(AH):
            out_ref[REACH + EDGE * h : REACH + EDGE * (h + 1)] = edge_ref[edge, h * KW : (h + 1) * KW]
        relative = (token_ref[:, side * 128 : (side + 1) * 128] - base).astype(F32)
        out_ref[INFO : INFO + 16] = jnp.broadcast_to(relative, (16, 128)).astype(BF16)
    copies[3].wait()
    weights = pair_w_ref[...]
    for side, out_ref in enumerate((down_ref, up_ref)):
        copies[4 + side].wait()
        rows = ordered(pair_ref, side, orders[side])
        out = lax.dot_general(weights, rows, NT, preferred_element_type=F32).astype(BF16)
        for k in range(8):
            out_ref[PAIR + 32 * k : PAIR + 32 * (k + 1)] = out[:, 128 * k : 128 * (k + 1)]
    for copy in copies[6:]:
        copy.wait()


def bias_kernel(pair_ref, pair_w_ref, token_ref, bias0_ref, bias1_ref, pick_ref, mask_ref):
    starts = chunk_starts(lax.axis_index("tok"))
    weights = pair_w_ref[...]
    for t in range(TOKD):
        rows = ordered(pair_ref, t, starts)
        out = lax.dot_general(weights, rows, NT, preferred_element_type=F32).astype(BF16)
        bias0_ref[t * H : (t + 1) * H] = out[:H]
        bias1_ref[t * H : (t + 1) * H] = out[H:]
    member = (token_ref[...] - lax.axis_index("tok") * TOKD == wanted_tokens()).astype(F32)
    member = jnp.concatenate([member, jnp.zeros((128 - ROWS, ATOMD), F32)], axis=0)
    pick_ref[...] = member.T.astype(BF16)
    mask_ref[...] = head_mask().astype(F32).astype(BF16)


def windowed(proj_ref, k_row, q_row, count, bias, first_atom):
    head_of_lane = lax.broadcasted_iota(jnp.int32, (1, CA), 1) // (CA // AH)
    queries = proj_ref[q_row : q_row + count, :CA]
    keys = proj_ref[k_row : k_row + KW, CA : 2 * CA]
    values = proj_ref[k_row : k_row + KW, 2 * CA :]
    stacked = jnp.concatenate(
        [jnp.where(head_of_lane == h, queries, jnp.zeros_like(queries)) for h in range(AH)], axis=0
    )
    scores = lax.dot_general(stacked, keys, NT, preferred_element_type=F32) * (CA // AH) ** (-0.5)
    scores = scores + jnp.concatenate(bias, axis=0).astype(F32)
    position = first_atom + k_row + lax.broadcasted_iota(jnp.int32, (1, KW), 1)
    inside = (position >= 0) & (position < 32 * ATOMD)
    scores = jnp.where(inside, scores, -1000000000.0)
    powers = jnp.exp(scores - jnp.max(scores, axis=-1, keepdims=True))
    total = jnp.sum(powers, axis=-1, keepdims=True)
    mixed = jnp.dot(powers.astype(BF16), values, preferred_element_type=F32) / total
    merged = jnp.where(head_of_lane == 0, mixed[:count], 0.0)
    for h in range(1, AH):
        merged = jnp.where(head_of_lane == h, mixed[h * count : (h + 1) * count], merged)
    return merged.astype(BF16)


def projected(rows, qkv_ref):
    normed = layer_norm(rows.astype(F32)).astype(BF16)
    return jnp.dot(normed, qkv_ref[...], preferred_element_type=F32).astype(BF16)


def own_bias(bias_ref, w):
    return [bias_ref[QW * w : QW * (w + 1), h * KW : (h + 1) * KW] for h in range(AH)]


def wanted_tokens():
    row = lax.broadcasted_iota(jnp.int32, (ROWS, 1), 0)
    return jnp.where(row < TOKD, row, jnp.where(row == TOKD, -1, jnp.where(row == TOKD + 1, TOKD, -200)))


def hidden_and_sums(hidden_in, mixed, relative, out_w_ref, agg_ref):
    hidden = (
        hidden_in.astype(F32) + jnp.dot(mixed, out_w_ref[...], preferred_element_type=F32)
    ).astype(BF16)
    lifted = jnp.maximum(jnp.dot(hidden, agg_ref[...], preferred_element_type=F32), 0.0)
    member = (relative == wanted_tokens()).astype(F32)
    counts = jnp.sum(member, axis=-1, keepdims=True)
    picker = member.astype(BF16)
    upper = lifted.astype(BF16)
    lower = (lifted - upper.astype(F32)).astype(BF16)
    sums = jnp.dot(picker, upper, preferred_element_type=F32)
    sums = sums + jnp.dot(picker, lower, preferred_element_type=F32)
    return hidden, sums, counts


def inner_atom_kernel(single_ref, bias_ref, token_ref, qkv_ref, out_w_ref, agg_ref,
                      proj_ref, hidden_ref, sums_ref, counts_ref, mixed_ref):
    tok = lax.axis_index("tok")
    proj_ref[...] = projected(single_ref[...], qkv_ref)
    for i, w in enumerate((4, 5, 2, 3)):
        mixed_ref[QW * i : QW * (i + 1)] = windowed(
            proj_ref, QW * w - HALO, QW * w, QW, own_bias(bias_ref, w), tok * ATOMD
        )
    lane = lax.broadcasted_iota(jnp.int32, (1, 128), 1)
    relative = jnp.where(lane < 64, token_ref[:, 128:], token_ref[:, :128]) - tok * TOKD
    hidden_in = jnp.concatenate([single_ref[128:192], single_ref[64:128]], axis=0)
    hidden, sums, counts = hidden_and_sums(hidden_in, mixed_ref[...], relative, out_w_ref, agg_ref)
    hidden_ref[:64] = hidden[64:]
    hidden_ref[64:] = hidden[:64]
    sums_ref[...] = sums
    counts_ref[...] = jnp.broadcast_to(counts, counts_ref.shape)


def atom_kernel(single_ref, lower_ref, upper_ref, bias_ref, token_ref, qkv_ref, out_w_ref, agg_ref,
                inner_ref, inner_hidden_ref, inner_sums_ref, inner_counts_ref,
                hidden_ref, stream_ref, normed_ref, own_ref, edge0_ref, edge1_ref, proj_ref, mixed_ref):
    tok = lax.axis_index("tok")
    first_atom = tok * ATOMD - REACH
    beside = projected(jnp.concatenate([lower_ref[:REACH], upper_ref[:REACH]], axis=0), qkv_ref)
    proj_ref[:REACH] = beside[:REACH]
    proj_ref[REACH : REACH + ATOMD] = inner_ref[...]
    proj_ref[REACH + ATOMD :] = beside[REACH:]
    mixed_ref[128 + EDGE : 256 - EDGE] = jnp.zeros((128 - 2 * EDGE, CA), BF16)
    for i, w in enumerate((0, 1, 6, 7)):
        mixed_ref[QW * i : QW * (i + 1)] = windowed(
            proj_ref, 32 + QW * w, REACH + QW * w, QW, own_bias(bias_ref, w), first_atom
        )
    for out_row, q_row, k_row, ref in (
        (128, REACH + ATOMD, 288, upper_ref), (256 - EDGE, REACH - EDGE, 0, lower_ref)
    ):
        bias = [ref[REACH + EDGE * h : REACH + EDGE * (h + 1)] for h in range(AH)]
        mixed_ref[out_row : out_row + EDGE] = windowed(proj_ref, k_row, q_row, EDGE, bias, first_atom)
    hidden_in = jnp.concatenate(
        [
            single_ref[:64],
            single_ref[192:],
            upper_ref[:EDGE],
            jnp.zeros((128 - 2 * EDGE, CA), BF16),
            lower_ref[REACH - EDGE : REACH],
        ],
        axis=0,
    )
    lane = lax.broadcasted_iota(jnp.int32, (1, 128), 1)
    after = upper_ref[INFO : INFO + 16][:1].astype(F32).astype(jnp.int32) + TOKD
    before = lower_ref[INFO : INFO + 16][:1].astype(F32).astype(jnp.int32) - TOKD
    near = jnp.where(lane < EDGE, after, jnp.where(lane >= 128 - EDGE, before, -100))
    outer = jnp.where(lane < 64, token_ref[:, :128], token_ref[:, 128:]) - tok * TOKD
    hidden, sums, counts = hidden_and_sums(
        hidden_in, mixed_ref[...], jnp.concatenate([outer, near], axis=1), out_w_ref, agg_ref
    )
    hidden_ref[:64] = hidden[:64]
    hidden_ref[64:192] = inner_hidden_ref[...]
    hidden_ref[192:] = hidden[64:128]
    stream = (sums + inner_sums_ref[...]) / jnp.maximum(counts + inner_counts_ref[:, :1], 1.0)
    stream_ref[...] = stream
    out = layer_norm(stream).astype(BF16)
    normed_ref[...] = out
    own_ref[...] = out[:TOKD]
    for block, ref in enumerate((edge0_ref, edge1_ref)):
        for side, source in enumerate((lower_ref, upper_ref)):
            for k in range(8):
                first = PAIR + 32 * k + H * block
                ref[H * side : H * (side + 1), 128 * k : 128 * (k + 1)] = source[first : first + H]


def head_mask():
    row = lax.broadcasted_iota(jnp.int32, (QROWS, 1), 0)
    lane = lax.broadcasted_iota(jnp.int32, (1, C), 1)
    start = (row & (H - 1)) * HEAD
    return (lane >= start) & (lane < start + HEAD)


def query_kernel(layer, normed_ref, qkv_ref, out_ref):
    queries = jnp.dot(normed_ref[...], qkv_ref[layer, :, :C], preferred_element_type=F32).astype(BF16)
    row = lax.broadcasted_iota(jnp.int32, (QROWS, ROWS), 0)
    column = lax.broadcasted_iota(jnp.int32, (QROWS, ROWS), 1)
    spread = ((row >> 4) == column).astype(F32).astype(BF16)
    repeated = jnp.dot(spread, queries, preferred_element_type=F32)
    repeated = jnp.where(head_mask(), repeated, 0.0).astype(BF16)
    lifted = lax.dot_general(repeated, qkv_ref[layer, :, C : 2 * C], NT, preferred_element_type=F32)
    out_ref[...] = (lifted * HEAD ** (-0.5)).astype(BF16)


def join_kernel(count, *refs):
    out_ref = refs[-1]
    rows = out_ref.shape[0] // 4
    for i, place in enumerate((0, 1, 3, 2)):
        out_ref[place * rows : (place + 1) * rows] = refs[i][...]


def tree(combine, parts):
    while len(parts) > 1:
        parts = [combine(*parts[i : i + 2]) if len(parts[i : i + 2]) == 2 else parts[i] for i in range(0, len(parts), 2)]
    return parts[0]


def along(reduce, values):
    return jnp.broadcast_to(reduce(values, axis=-1, keepdims=True), values.shape)


def scored(query_ref, rows_ref, bias_ref, edge_bias_ref, half):
    scores = lax.dot_general(query_ref[...], rows_ref[...], NT, preferred_element_type=F32)
    parts = []
    for k in range(HALF // 128):
        lanes = slice(half * HALF + 128 * k, half * HALF + 128 * (k + 1))
        bias = jnp.concatenate([bias_ref[:, lanes], edge_bias_ref[:, lanes]], axis=0)
        parts.append(scores[:, 128 * k : 128 * (k + 1)] + bias.astype(F32))
    return parts


def weighted(powers, rows_ref):
    weights = jnp.concatenate([part.astype(BF16) for part in powers], axis=1)
    return jnp.dot(weights, rows_ref[...], preferred_element_type=F32)


def near_kernel(query_ref, near_ref, bias_ref, edge_bias_ref, mixed_ref, maximum_ref, total_ref):
    scores = scored(query_ref, near_ref, bias_ref, edge_bias_ref, 0)
    maximum = along(jnp.max, tree(jnp.maximum, scores))
    powers = [jnp.exp(part - maximum) for part in scores]
    maximum_ref[...] = maximum
    total_ref[...] = tree(jnp.add, powers)
    mixed_ref[...] = weighted(powers, near_ref)


def attend(layer, query_ref, far_ref, bias_ref, edge_bias_ref, mixed_ref, maximum_ref, total_ref, mask_ref,
           qkv_ref, out_w_ref, stream_ref):
    scores = scored(query_ref, far_ref, bias_ref, edge_bias_ref, 1)
    maximum = jnp.maximum(maximum_ref[...], along(jnp.max, tree(jnp.maximum, scores)))
    powers = [jnp.exp(part - maximum) for part in scores]
    fade = jnp.exp(maximum_ref[...] - maximum)
    share = 1.0 / along(jnp.sum, total_ref[...] * fade + tree(jnp.add, powers))
    fade = fade * share
    new = weighted(powers, far_ref)
    mixed = jnp.concatenate(
        [
            (mixed_ref[:, 128 * k : 128 * (k + 1)] * fade + new[:, 128 * k : 128 * (k + 1)] * share).astype(BF16)
            for k in range(C // 128)
        ],
        axis=1,
    )
    valued = jnp.dot(mixed, qkv_ref[layer, :, 2 * C :], preferred_element_type=F32).astype(BF16) * mask_ref[...]
    row = lax.broadcasted_iota(jnp.int32, (ROWS, QROWS), 0)
    column = lax.broadcasted_iota(jnp.int32, (ROWS, QROWS), 1)
    gather = ((column >> 4) == row).astype(F32).astype(BF16)
    heads = jnp.dot(gather, valued, preferred_element_type=F32).astype(BF16)
    return stream_ref[...] + jnp.dot(heads, out_w_ref[layer], preferred_element_type=F32)


def middle_kernel(*refs):
    stream_ref, normed_ref, own_ref = refs[11:]
    stream = attend(0, *refs[:11])
    stream_ref[...] = stream
    out = layer_norm(stream).astype(BF16)
    normed_ref[...] = out
    own_ref[...] = out[:TOKD]


def last_kernel(*refs):
    bcast_ref, pick_ref, hidden_ref, atom_out_ref, token_out_ref = refs[11:]
    token_out = attend(1, *refs[:11]).astype(BF16)
    token_out_ref[...] = token_out[:TOKD]
    carry = jnp.dot(token_out, bcast_ref[...], preferred_element_type=F32).astype(BF16)
    picked = jnp.dot(pick_ref[:, :ROWS], carry, preferred_element_type=F32)
    atom_out_ref[...] = (hidden_ref[...].astype(F32) + picked).astype(BF16)


def flips(dx, dy, dc):
    pairs = []
    for tok in range(32):
        core, y, x = tok % 2, (tok // 2) % 4, tok // 8
        pairs.append((tok, ((x ^ dx) * 4 + (y ^ dy)) * 2 + (core ^ dc)))
    return pairs


def crossed(k, first):
    along_y, along_x = flips(0, k, 0), flips(k, 0, 0)
    return [
        (along_y if (tok % 2 == 0) == first else along_x)[tok] for tok in range(32)
    ]


def join(pieces, after):
    return pl.pallas_call(
        functools.partial(join_kernel, len(after)),
        in_specs=[VMEM] * 4 + [pl.BlockSpec(memory_space=pl.ANY)] * len(after),
        out_specs=VMEM,
        out_shape=shape(4 * pieces[0].shape[0], C),
        compiler_params=params(4),
        name="join",
    )(*pieces, *after)


def exchange(rows, first):
    return [rows] + [lax.ppermute(rows, "tok", crossed(k, first)) for k in (1, 3, 2)]


def in_hbm(*arrays):
    return [pltpu.with_memory_space_constraint(x, pltpu.HBM) for x in arrays]


def shape(rows, columns, dtype=BF16):
    return jax.ShapeDtypeStruct((rows, columns), dtype)


def local(atom_single, atom_bias, atom_token, atom_counts, pair_rep, atom_qkv_w, atom_out_w, agg_w,
          tok_qkv_w, tok_out_w, pair_w, bcast_w):
    tokens = atom_token.reshape(1, ATOMD)
    pair_wt = pair_w.T
    hbm = pl.BlockSpec(memory_space=pltpu.HBM)

    small = (atom_single, atom_bias, tokens, atom_qkv_w, atom_out_w, agg_w)
    to_down, to_up, *small = pl.pallas_call(
        pack_kernel,
        in_specs=[hbm] * 8,
        out_specs=[VMEM] * 8,
        out_shape=[shape(PACK, CA)] * 2 + [jax.ShapeDtypeStruct(x.shape, x.dtype) for x in small],
        scratch_shapes=[
            pltpu.VMEM((2, KEYS, 128), BF16),
            pltpu.VMEM((32, 128), BF16),
            pltpu.SemaphoreType.DMA((9,)),
        ],
        compiler_params=params(8),
        name="pack",
    )(*in_hbm(*small, pair_rep, pair_wt))
    from_upper = lax.ppermute(to_down, "tok", [((i + 1) % 32, i) for i in range(32)])
    from_lower = lax.ppermute(to_up, "tok", [(i, (i + 1) % 32) for i in range(32)])

    *bias, pick, mask = pl.pallas_call(
        bias_kernel,
        in_specs=[VMEM] * 3,
        out_specs=[VMEM] * 4,
        out_shape=[shape(TOKD * H, KEYS)] * 2 + [shape(ATOMD, 128), shape(QROWS, C)],
        compiler_params=params(12),
        cost_estimate=pl.CostEstimate(flops=2 * 32 * 1024 * 128 * 32, bytes_accessed=10 * 2**20, transcendentals=0),
        name="bias",
    )(pair_rep, pair_wt, small[2])

    inner = pl.pallas_call(
        inner_atom_kernel,
        in_specs=[VMEM] * 6,
        out_specs=[VMEM] * 4,
        out_shape=[
            shape(ATOMD, 3 * CA),
            shape(4 * QW, CA),
            shape(ROWS, C, F32),
            shape(ROWS, 128, F32),
        ],
        scratch_shapes=[pltpu.VMEM((4 * QW, CA), BF16)],
        compiler_params=params(8),
        cost_estimate=pl.CostEstimate(flops=10**9, bytes_accessed=5 * 2**20, transcendentals=0),
        name="inner_atoms",
    )(*small)
    hidden, stream, normed, own, *edge_bias = pl.pallas_call(
        atom_kernel,
        in_specs=[VMEM] * 12,
        out_specs=[VMEM] * 6,
        out_shape=[shape(ATOMD, CA), shape(ROWS, C, F32), shape(ROWS, C), shape(TOKD, C)] + [shape(2 * H, KEYS)] * 2,
        scratch_shapes=[pltpu.VMEM((2 * REACH + ATOMD, 3 * CA), BF16), pltpu.VMEM((256, CA), BF16)],
        compiler_params=params(8),
        name="atoms",
    )(small[0], from_lower, from_upper, *small[1:], *inner)

    for layer in range(2):
        pieces = exchange(own, True)
        queries = pl.pallas_call(
            functools.partial(query_kernel, layer),
            in_specs=[VMEM] * 2,
            out_specs=VMEM,
            out_shape=shape(QROWS, C),
            compiler_params=params(16),
            cost_estimate=pl.CostEstimate(flops=10**9, bytes_accessed=5 * 2**20, transcendentals=0),
            name="queries",
        )(normed, tok_qkv_w)
        pieces = exchange(join(pieces, [queries]), False)
        near = join(pieces, [bias[0]] if layer == 0 else [])
        far = lax.ppermute(near, "tok", flips(0, 0, 1))
        partial = pl.pallas_call(
            near_kernel,
            in_specs=[VMEM] * 4,
            out_specs=[VMEM] * 3,
            out_shape=[shape(QROWS, C, F32)] + [shape(QROWS, 128, F32)] * 2,
            compiler_params=params(16),
            cost_estimate=pl.CostEstimate(flops=2 * 10**9, bytes_accessed=5 * 2**20, transcendentals=300000),
            name="near",
        )(queries, near, bias[layer], edge_bias[layer])
        operands = (queries, far, bias[layer], edge_bias[layer], *partial, mask, tok_qkv_w, tok_out_w, stream)
        if layer == 0:
            stream, normed, own = pl.pallas_call(
                middle_kernel,
                in_specs=[VMEM] * 11,
                out_specs=[VMEM] * 3,
                out_shape=[shape(ROWS, C, F32), shape(ROWS, C), shape(TOKD, C)],
                compiler_params=params(16),
                name="block",
            )(*operands)
        else:
            atom_out, token_out = pl.pallas_call(
                last_kernel,
                in_specs=[VMEM] * 14,
                out_specs=[VMEM] * 2,
                out_shape=[shape(ATOMD, CA), shape(TOKD, C)],
                compiler_params=params(16),
                name="block_and_broadcast",
            )(*operands, bcast_w, pick, hidden)
    return (atom_out, token_out)


def solution(mesh):
    placed = (
        P(("seed", "tok"), None),
        P("tok", None),
        P("tok"),
        P("tok"),
        P("tok", None, None),
        P(),
        P(),
        P(),
        P(),
        P(),
        P(),
        P(),
    )
    return jax.shard_map(
        local,
        mesh=mesh,
        in_specs=placed,
        out_specs=(P(("seed", "tok"), None), P(("seed", "tok"), None)),
        check_vma=False,
    )
```

```python
import functools

import jax
import jax.numpy as jnp
from jax import lax
from jax.experimental import pallas as pl
from jax.experimental.pallas import tpu as pltpu
from jax.sharding import PartitionSpec as P

C = 768
H = 16
HEAD = C // H
CA = 128
AH = 4
QW = 32
KW = 128
HALO = 48
NB = 2
EDGE = 16
REACH = EDGE + 64
TOKD = 32
ATOMD = 256
ROWS = 48
QROWS = 34 * H
KEYS = 1024
HALF = 512
CHUNK = 32
INFO = REACH + AH * EDGE
PACK = INFO + 16
F32 = jnp.float32
BF16 = jnp.bfloat16

NT = (((1,), (1,)), ((), ()))


def params(mib):
    return pltpu.CompilerParams(vmem_limit_bytes=mib * 1024 * 1024)


VMEM = pl.BlockSpec(memory_space=pltpu.VMEM)


def layer_norm(values):
    average = jnp.mean(values, axis=-1, keepdims=True)
    centred = values - average
    variance = jnp.mean(centred * centred, axis=-1, keepdims=True)
    return centred * lax.rsqrt(variance + 1e-05)


def tree(combine, parts):
    while len(parts) > 1:
        parts = [combine(*parts[i : i + 2]) if len(parts[i : i + 2]) == 2 else parts[i] for i in range(0, len(parts), 2)]
    return parts[0]


def along(reduce, values):
    return jnp.broadcast_to(reduce(values, axis=-1, keepdims=True), values.shape)


def chunk_starts(tok):
    core, y, x = lax.rem(tok, 2), lax.rem(tok // 2, 4), tok // 8
    starts = []
    for j in range(32):
        slow, fast = (j % 16) // 4, j % 4
        plane = core if j < 16 else 1 - core
        kx = jnp.where(plane == 0, slow, fast)
        ky = jnp.where(plane == 0, fast, slow)
        starts.append((((x ^ kx) * 4 + (y ^ ky)) * 2 + plane) * CHUNK)
    return starts


def ordered(pair_ref, t, starts):
    return jnp.concatenate(
        [pair_ref[t, pl.ds(pl.multiple_of(s, CHUNK), CHUNK), :] for s in starts], axis=0
    )


def for_neighbours(core, apart_ref, beside_ref, fill):
    for first, refs in ((0, (apart_ref, beside_ref)), (1, (beside_ref, apart_ref))):
        @pl.when(core == first)
        def _():
            for side, ref in enumerate(refs):
                fill(side, ref)


def pack_kernel(*refs):
    sources, targets, sems = refs[:6], refs[8:14], refs[14]
    apart_ref, beside_ref = refs[6:8]
    single_ref, edge_ref, token_ref = targets[:3]
    copies = [
        pltpu.make_async_copy(source, target, sems.at[i])
        for i, (source, target) in enumerate(zip(sources, targets))
    ]
    for copy in copies:
        copy.start()
    tok = lax.axis_index("tok")
    for copy in copies[:3]:
        copy.wait()

    def fill(side, out_ref):
        rows = slice(0, REACH) if side == 0 else slice(ATOMD - REACH, ATOMD)
        edge = slice(0, EDGE) if side == 0 else slice(ATOMD - EDGE, ATOMD)
        out_ref[:REACH] = single_ref[rows]
        for h in range(AH):
            out_ref[REACH + EDGE * h : REACH + EDGE * (h + 1)] = edge_ref[edge, h * KW : (h + 1) * KW]
        relative = (token_ref[:, side * 128 : (side + 1) * 128] - tok * TOKD).astype(F32)
        out_ref[INFO : INFO + 16] = jnp.broadcast_to(relative, (16, 128)).astype(BF16)

    for_neighbours(lax.rem(tok, 2), apart_ref, beside_ref, fill)
    for copy in copies[3:]:
        copy.wait()


def bias_kernel(pair_ref, pair_w_ref, bias0_ref, bias1_ref):
    starts = chunk_starts(lax.axis_index("tok"))
    weights = pair_w_ref[...]
    for t in range(TOKD):
        rows = ordered(pair_ref, t, starts)
        out = lax.dot_general(weights, rows, NT, preferred_element_type=F32).astype(BF16)
        bias0_ref[t * H : (t + 1) * H] = out[:H]
        bias1_ref[t * H : (t + 1) * H] = out[H:]


def windowed(proj_ref, windows, first_atom):
    head_of_lane = lax.broadcasted_iota(jnp.int32, (1, CA), 1) // (CA // AH)
    heads = [head_of_lane == h for h in range(AH)]
    lane = lax.broadcasted_iota(jnp.int32, (1, KW), 1)
    products = []
    for k_row, q_row, count, bias in windows:
        queries = proj_ref[q_row : q_row + count, :CA]
        stacked = jnp.concatenate([jnp.where(head, queries, jnp.zeros_like(queries)) for head in heads], axis=0)
        keys = proj_ref[k_row : k_row + KW, CA : 2 * CA]
        products.append(lax.dot_general(stacked, keys, NT, preferred_element_type=F32))
    scores = []
    for product, (k_row, q_row, count, bias) in zip(products, windows):
        position = first_atom + k_row + lane
        inside = (position >= 0) & (position < 32 * ATOMD)
        score = product * (CA // AH) ** (-0.5) + jnp.concatenate(bias, axis=0).astype(F32)
        scores.append(jnp.where(inside, score, -1000000000.0))
    scores = jnp.concatenate(scores, axis=0)
    powers = jnp.exp(scores - along(jnp.max, scores))
    share = 1.0 / along(jnp.sum, powers)
    weights = powers.astype(BF16)
    mixed = []
    first = 0
    for k_row, q_row, count, bias in windows:
        values = proj_ref[k_row : k_row + KW, 2 * CA :]
        rows = slice(first, first + AH * count)
        mixed.append(jnp.dot(weights[rows], values, preferred_element_type=F32) * share[rows])
        first += AH * count
    merged = []
    for rows, (k_row, q_row, count, bias) in zip(mixed, windows):
        out = jnp.where(heads[0], rows[:count], 0.0)
        for h in range(1, AH):
            out = jnp.where(heads[h], rows[h * count : (h + 1) * count], out)
        merged.append(out.astype(BF16))
    return merged


def projected(rows, qkv_ref):
    normed = layer_norm(rows.astype(F32)).astype(BF16)
    return jnp.dot(normed, qkv_ref[...], preferred_element_type=F32).astype(BF16)


def own_bias(bias_ref, w):
    return [bias_ref[QW * w : QW * (w + 1), h * KW : (h + 1) * KW] for h in range(AH)]


def wanted_tokens():
    row = lax.broadcasted_iota(jnp.int32, (ROWS, 1), 0)
    return jnp.where(row < TOKD, row, jnp.where(row == TOKD, -1, jnp.where(row == TOKD + 1, TOKD, -200)))


def hidden_and_sums(hidden_in, mixed, relative, out_w_ref, agg_ref):
    hidden = (
        hidden_in.astype(F32) + jnp.dot(mixed, out_w_ref[...], preferred_element_type=F32)
    ).astype(BF16)
    lifted = jnp.maximum(jnp.dot(hidden, agg_ref[...], preferred_element_type=F32), 0.0)
    member = (relative == wanted_tokens()).astype(F32)
    counts = jnp.sum(member, axis=-1, keepdims=True)
    picker = member.astype(BF16)
    upper = lifted.astype(BF16)
    lower = (lifted - upper.astype(F32)).astype(BF16)
    sums = jnp.dot(picker, upper, preferred_element_type=F32)
    sums = sums + jnp.dot(picker, lower, preferred_element_type=F32)
    return hidden, sums, counts


def inner_atom_kernel(single_ref, bias_ref, token_ref, qkv_ref, out_w_ref, agg_ref,
                      proj_ref, hidden_ref, sums_ref, counts_ref, pick_ref, mask_ref):
    tok = lax.axis_index("tok")
    proj_ref[...] = projected(single_ref[...], qkv_ref)
    windows = [(QW * w - HALO, QW * w, QW, own_bias(bias_ref, w)) for w in (4, 5, 2, 3)]
    mixed = jnp.concatenate(windowed(proj_ref, windows, tok * ATOMD), axis=0)
    lane = lax.broadcasted_iota(jnp.int32, (1, 128), 1)
    relative = jnp.where(lane < 64, token_ref[:, 128:], token_ref[:, :128]) - tok * TOKD
    hidden_in = jnp.concatenate([single_ref[128:192], single_ref[64:128]], axis=0)
    hidden, sums, counts = hidden_and_sums(hidden_in, mixed, relative, out_w_ref, agg_ref)
    hidden_ref[:64] = hidden[64:]
    hidden_ref[64:] = hidden[:64]
    sums_ref[...] = sums
    counts_ref[...] = jnp.broadcast_to(counts, counts_ref.shape)
    member = (token_ref[...] - tok * TOKD == wanted_tokens()).astype(F32)
    member = jnp.concatenate([member, jnp.zeros((128 - ROWS, ATOMD), F32)], axis=0)
    pick_ref[...] = member.T.astype(BF16)
    mask_ref[...] = head_mask().astype(F32).astype(BF16)


def atom_kernel(single_ref, apart_ref, beside_ref, bias_ref, token_ref, qkv_ref, out_w_ref, agg_ref,
                inner_ref, inner_hidden_ref, inner_sums_ref, inner_counts_ref,
                hidden_ref, stream_ref, normed_ref, own_ref, proj_ref, both_ref):
    tok = lax.axis_index("tok")
    core = lax.rem(tok, 2)
    both_ref[0] = apart_ref[...]
    both_ref[1] = beside_ref[...]
    lower_ref, upper_ref = both_ref.at[core], both_ref.at[1 - core]
    first_atom = tok * ATOMD - REACH
    beside = projected(jnp.concatenate([lower_ref[:REACH], upper_ref[:REACH]], axis=0), qkv_ref)
    proj_ref[:REACH] = beside[:REACH]
    proj_ref[REACH : REACH + ATOMD] = inner_ref[...]
    proj_ref[REACH + ATOMD :] = beside[REACH:]
    windows = [(32 + QW * w, REACH + QW * w, QW, own_bias(bias_ref, w)) for w in (0, 1, 6, 7)]
    for k_row, q_row, ref in ((288, REACH + ATOMD, upper_ref), (0, REACH - EDGE, lower_ref)):
        windows.append((k_row, q_row, EDGE, [ref[REACH + EDGE * h : REACH + EDGE * (h + 1)] for h in range(AH)]))
    mixed = windowed(proj_ref, windows, first_atom)
    mixed.insert(5, jnp.zeros((128 - 2 * EDGE, CA), BF16))
    hidden_in = jnp.concatenate(
        [
            single_ref[:64],
            single_ref[192:],
            upper_ref[:EDGE],
            jnp.zeros((128 - 2 * EDGE, CA), BF16),
            lower_ref[REACH - EDGE : REACH],
        ],
        axis=0,
    )
    lane = lax.broadcasted_iota(jnp.int32, (1, 128), 1)
    after = upper_ref[INFO : INFO + 16][:1].astype(F32).astype(jnp.int32) + TOKD
    before = lower_ref[INFO : INFO + 16][:1].astype(F32).astype(jnp.int32) - TOKD
    near = jnp.where(lane < EDGE, after, jnp.where(lane >= 128 - EDGE, before, -100))
    outer = jnp.where(lane < 64, token_ref[:, :128], token_ref[:, 128:]) - tok * TOKD
    hidden, sums, counts = hidden_and_sums(
        hidden_in, jnp.concatenate(mixed, axis=0), jnp.concatenate([outer, near], axis=1), out_w_ref, agg_ref
    )
    hidden_ref[:64] = hidden[:64]
    hidden_ref[64:192] = inner_hidden_ref[...]
    hidden_ref[192:] = hidden[64:128]
    stream = (sums + inner_sums_ref[...]) / jnp.maximum(counts + inner_counts_ref[:, :1], 1.0)
    stream_ref[...] = stream
    out = layer_norm(stream).astype(BF16)
    normed_ref[...] = out
    own_ref[...] = out[:TOKD]


def head_mask():
    row = lax.broadcasted_iota(jnp.int32, (QROWS, 1), 0)
    lane = lax.broadcasted_iota(jnp.int32, (1, C), 1)
    start = (row & (H - 1)) * HEAD
    return (lane >= start) & (lane < start + HEAD)


def query_kernel(layer, normed_ref, qkv_ref, out_ref):
    queries = jnp.dot(normed_ref[...], qkv_ref[layer, :, :C], preferred_element_type=F32).astype(BF16)
    row = lax.broadcasted_iota(jnp.int32, (QROWS, ROWS), 0)
    column = lax.broadcasted_iota(jnp.int32, (QROWS, ROWS), 1)
    spread = ((row >> 4) == column).astype(F32).astype(BF16)
    repeated = jnp.dot(spread, queries, preferred_element_type=F32)
    repeated = jnp.where(head_mask(), repeated, 0.0).astype(BF16)
    lifted = lax.dot_general(repeated, qkv_ref[layer, :, C : 2 * C], NT, preferred_element_type=F32)
    out_ref[...] = (lifted * HEAD ** (-0.5)).astype(BF16)


def first_query_kernel(normed_ref, qkv_ref, pair_hbm, pair_w_hbm, out_ref, apart_ref, beside_ref,
                       pair_ref, pair_w_ref, sems):
    copies = [
        pltpu.make_async_copy(pair_w_hbm, pair_w_ref, sems.at[0]),
        pltpu.make_async_copy(pair_hbm.at[0], pair_ref.at[0], sems.at[1]),
        pltpu.make_async_copy(pair_hbm.at[TOKD - 1], pair_ref.at[1], sems.at[2]),
    ]
    for copy in copies:
        copy.start()
    query_kernel(0, normed_ref, qkv_ref, out_ref)
    for copy in copies:
        copy.wait()
    tok = lax.axis_index("tok")
    outs = []
    for side, owner in enumerate((jnp.maximum(tok - 1, 0), jnp.minimum(tok + 1, 31))):
        rows = ordered(pair_ref, side, chunk_starts(owner))
        outs.append(lax.dot_general(pair_w_ref[...], rows, NT, preferred_element_type=F32).astype(BF16))

    def fill(side, ref):
        ref[...] = outs[side]

    for_neighbours(lax.rem(tok, 2), apart_ref, beside_ref, fill)


def join_edges_kernel(*refs):
    join_kernel(0, *refs[:4], refs[7])
    both_ref = refs[10]
    both_ref[0] = refs[4][...]
    both_ref[1] = refs[5][...]
    core = lax.rem(lax.axis_index("tok"), 2)
    for block, ref in enumerate(refs[8:10]):
        for side, index in enumerate((core, 1 - core)):
            ref[side * H : (side + 1) * H] = both_ref[index, block * H : (block + 1) * H]


def join_kernel(count, *refs):
    out_ref = refs[-1]
    rows = out_ref.shape[0] // 4
    for i, place in enumerate((0, 1, 3, 2)):
        out_ref[place * rows : (place + 1) * rows] = refs[i][...]


def scored(query_ref, rows_ref, bias_ref, edge_bias_ref, half):
    scores = lax.dot_general(query_ref[...], rows_ref[...], NT, preferred_element_type=F32)
    parts = []
    for k in range(HALF // 128):
        lanes = slice(half * HALF + 128 * k, half * HALF + 128 * (k + 1))
        bias = jnp.concatenate([bias_ref[:, lanes], edge_bias_ref[:, lanes]], axis=0)
        parts.append(scores[:, 128 * k : 128 * (k + 1)] + bias.astype(F32))
    return parts


def weighted(powers, rows_ref):
    weights = jnp.concatenate([part.astype(BF16) for part in powers], axis=1)
    return jnp.dot(weights, rows_ref[...], preferred_element_type=F32)


def near_kernel(query_ref, near_ref, bias_ref, edge_bias_ref, mixed_ref, maximum_ref, total_ref):
    scores = scored(query_ref, near_ref, bias_ref, edge_bias_ref, 0)
    maximum = along(jnp.max, tree(jnp.maximum, scores))
    powers = [jnp.exp(part - maximum) for part in scores]
    maximum_ref[...] = maximum
    total_ref[...] = tree(jnp.add, powers)
    mixed_ref[...] = weighted(powers, near_ref)


def attend(layer, query_ref, far_ref, bias_ref, edge_bias_ref, mixed_ref, maximum_ref, total_ref, mask_ref,
           qkv_ref, out_w_ref, stream_ref):
    scores = scored(query_ref, far_ref, bias_ref, edge_bias_ref, 1)
    maximum = jnp.maximum(maximum_ref[...], along(jnp.max, tree(jnp.maximum, scores)))
    powers = [jnp.exp(part - maximum) for part in scores]
    fade = jnp.exp(maximum_ref[...] - maximum)
    share = 1.0 / along(jnp.sum, total_ref[...] * fade + tree(jnp.add, powers))
    fade = fade * share
    new = weighted(powers, far_ref)
    mixed = jnp.concatenate(
        [
            (mixed_ref[:, 128 * k : 128 * (k + 1)] * fade + new[:, 128 * k : 128 * (k + 1)] * share).astype(BF16)
            for k in range(C // 128)
        ],
        axis=1,
    )
    valued = jnp.dot(mixed, qkv_ref[layer, :, 2 * C :], preferred_element_type=F32).astype(BF16) * mask_ref[...]
    row = lax.broadcasted_iota(jnp.int32, (ROWS, QROWS), 0)
    column = lax.broadcasted_iota(jnp.int32, (ROWS, QROWS), 1)
    gather = ((column >> 4) == row).astype(F32).astype(BF16)
    heads = jnp.dot(gather, valued, preferred_element_type=F32).astype(BF16)
    return stream_ref[...] + jnp.dot(heads, out_w_ref[layer], preferred_element_type=F32)


def middle_kernel(*refs):
    stream_ref, normed_ref, own_ref = refs[11:]
    stream = attend(0, *refs[:11])
    stream_ref[...] = stream
    out = layer_norm(stream).astype(BF16)
    normed_ref[...] = out
    own_ref[...] = out[:TOKD]


def last_kernel(*refs):
    bcast_ref, pick_ref, hidden_ref, atom_out_ref, token_out_ref = refs[11:]
    token_out = attend(1, *refs[:11]).astype(BF16)
    token_out_ref[...] = token_out[:TOKD]
    carry = jnp.dot(token_out, bcast_ref[...], preferred_element_type=F32).astype(BF16)
    picked = jnp.dot(pick_ref[:, :ROWS], carry, preferred_element_type=F32)
    atom_out_ref[...] = (hidden_ref[...].astype(F32) + picked).astype(BF16)


def flips(dx, dy, dc):
    pairs = []
    for tok in range(32):
        core, y, x = tok % 2, (tok // 2) % 4, tok // 8
        pairs.append((tok, ((x ^ dx) * 4 + (y ^ dy)) * 2 + (core ^ dc)))
    return pairs


def crossed(k, first):
    along_y, along_x = flips(0, k, 0), flips(k, 0, 0)
    return [
        (along_y if (tok % 2 == 0) == first else along_x)[tok] for tok in range(32)
    ]


def join(pieces, after):
    return pl.pallas_call(
        functools.partial(join_kernel, len(after)),
        in_specs=[VMEM] * 4 + [pl.BlockSpec(memory_space=pl.ANY)] * len(after),
        out_specs=VMEM,
        out_shape=shape(4 * pieces[0].shape[0], C),
        compiler_params=params(4),
        name="join",
    )(*pieces, *after)


def exchange(rows, first):
    return [rows] + [lax.ppermute(rows, "tok", crossed(k, first)) for k in (1, 3, 2)]


def in_hbm(*arrays):
    return [pltpu.with_memory_space_constraint(x, pltpu.HBM) for x in arrays]


def shape(rows, columns, dtype=BF16):
    return jax.ShapeDtypeStruct((rows, columns), dtype)


def local(atom_single, atom_bias, atom_token, atom_counts, pair_rep, atom_qkv_w, atom_out_w, agg_w,
          tok_qkv_w, tok_out_w, pair_w, bcast_w):
    tokens = atom_token.reshape(1, ATOMD)
    pair_wt = pair_w.T
    hbm = pl.BlockSpec(memory_space=pltpu.HBM)

    small = (atom_single, atom_bias, tokens, atom_qkv_w, atom_out_w, agg_w)
    to_apart, to_beside, *small = pl.pallas_call(
        pack_kernel,
        in_specs=[hbm] * 6,
        out_specs=[VMEM] * 8,
        out_shape=[shape(PACK, CA)] * 2 + [jax.ShapeDtypeStruct(x.shape, x.dtype) for x in small],
        scratch_shapes=[pltpu.SemaphoreType.DMA((6,))],
        compiler_params=params(8),
        cost_estimate=pl.CostEstimate(flops=4 * 10**9, bytes_accessed=16 * 2**20, transcendentals=0),
        name="pack",
    )(*in_hbm(*small))
    across = [(i, (i + (1 if i % 2 else -1)) % 32) for i in range(32)]
    apart = lax.ppermute(to_apart, "tok", across)
    beside = lax.ppermute(to_beside, "tok", flips(0, 0, 1))

    bias = pl.pallas_call(
        bias_kernel,
        in_specs=[VMEM] * 2,
        out_specs=[VMEM] * 2,
        out_shape=[shape(TOKD * H, KEYS)] * 2,
        compiler_params=params(12),
        cost_estimate=pl.CostEstimate(flops=2 * 32 * 1024 * 128 * 32, bytes_accessed=10 * 2**20, transcendentals=0),
        name="bias",
    )(pair_rep, pair_wt)

    *inner, pick, mask = pl.pallas_call(
        inner_atom_kernel,
        in_specs=[VMEM] * 6,
        out_specs=[VMEM] * 6,
        out_shape=[
            shape(ATOMD, 3 * CA),
            shape(4 * QW, CA),
            shape(ROWS, C, F32),
            shape(ROWS, 128, F32),
            shape(ATOMD, 128),
            shape(QROWS, C),
        ],
        compiler_params=params(8),
        cost_estimate=pl.CostEstimate(flops=4 * 10**9, bytes_accessed=16 * 2**20, transcendentals=0),
        name="inner_atoms",
    )(*small)
    hidden, stream, normed, own = pl.pallas_call(
        atom_kernel,
        in_specs=[VMEM] * 12,
        out_specs=[VMEM] * 4,
        out_shape=[shape(ATOMD, CA), shape(ROWS, C, F32), shape(ROWS, C), shape(TOKD, C)],
        scratch_shapes=[pltpu.VMEM((2 * REACH + ATOMD, 3 * CA), BF16), pltpu.VMEM((2, PACK, CA), BF16)],
        compiler_params=params(8),
        cost_estimate=pl.CostEstimate(flops=4 * 10**9, bytes_accessed=16 * 2**20, transcendentals=0),
        name="atoms",
    )(small[0], apart, beside, *small[1:], *inner)

    for layer in range(2):
        pieces = exchange(own, True)
        if layer == 0:
            queries, *edges = pl.pallas_call(
                first_query_kernel,
                in_specs=[VMEM] * 2 + [hbm] * 2,
                out_specs=[VMEM] * 3,
                out_shape=[shape(QROWS, C)] + [shape(NB * H, KEYS)] * 2,
                scratch_shapes=[
                    pltpu.VMEM((2, KEYS, 128), BF16),
                    pltpu.VMEM((32, 128), BF16),
                    pltpu.SemaphoreType.DMA((3,)),
                ],
                compiler_params=params(16),
                cost_estimate=pl.CostEstimate(flops=10**9, bytes_accessed=5 * 2**20, transcendentals=0),
                name="queries",
            )(normed, tok_qkv_w, *in_hbm(pair_rep, pair_wt))
            edges = [lax.ppermute(edges[0], "tok", across), lax.ppermute(edges[1], "tok", flips(0, 0, 1))]
        else:
            queries = pl.pallas_call(
                functools.partial(query_kernel, layer),
                in_specs=[VMEM] * 2,
                out_specs=VMEM,
                out_shape=shape(QROWS, C),
                compiler_params=params(16),
                cost_estimate=pl.CostEstimate(flops=10**9, bytes_accessed=5 * 2**20, transcendentals=0),
                name="queries",
            )(normed, tok_qkv_w)
        pieces = exchange(join(pieces, [queries]), False)
        if layer == 0:
            near, *edge_bias = pl.pallas_call(
                join_edges_kernel,
                in_specs=[VMEM] * 6 + [pl.BlockSpec(memory_space=pl.ANY)],
                out_specs=[VMEM] * 3,
                out_shape=[shape(HALF, C)] + [shape(2 * H, KEYS)] * 2,
                scratch_shapes=[pltpu.VMEM((2, NB * H, KEYS), BF16)],
                compiler_params=params(8),
                name="join",
            )(*pieces, *edges, bias[0])
        else:
            near = join(pieces, [])
        far = lax.ppermute(near, "tok", flips(0, 0, 1))
        partial = pl.pallas_call(
            near_kernel,
            in_specs=[VMEM] * 4,
            out_specs=[VMEM] * 3,
            out_shape=[shape(QROWS, C, F32)] + [shape(QROWS, 128, F32)] * 2,
            compiler_params=params(16),
            cost_estimate=pl.CostEstimate(flops=2 * 10**9, bytes_accessed=5 * 2**20, transcendentals=300000),
            name="near",
        )(queries, near, bias[layer], edge_bias[layer])
        operands = (queries, far, bias[layer], edge_bias[layer], *partial, mask, tok_qkv_w, tok_out_w, stream)
        if layer == 0:
            stream, normed, own = pl.pallas_call(
                middle_kernel,
                in_specs=[VMEM] * 11,
                out_specs=[VMEM] * 3,
                out_shape=[shape(ROWS, C, F32), shape(ROWS, C), shape(TOKD, C)],
                compiler_params=params(16),
                name="block",
            )(*operands)
        else:
            atom_out, token_out = pl.pallas_call(
                last_kernel,
                in_specs=[VMEM] * 14,
                out_specs=[VMEM] * 2,
                out_shape=[shape(ATOMD, CA), shape(TOKD, C)],
                compiler_params=params(16),
                name="block_and_broadcast",
            )(*operands, bcast_w, pick, hidden)
    return (atom_out, token_out)


def solution(mesh):
    placed = (
        P(("seed", "tok"), None),
        P("tok", None),
        P("tok"),
        P("tok"),
        P("tok", None, None),
        P(),
        P(),
        P(),
        P(),
        P(),
        P(),
        P(),
    )
    return jax.shard_map(
        local,
        mesh=mesh,
        in_specs=placed,
        out_specs=(P(("seed", "tok"), None), P(("seed", "tok"), None)),
        check_vma=False,
    )
```

```python
import functools

import jax
import jax.numpy as jnp
from jax import lax
from jax.experimental import pallas as pl
from jax.experimental.pallas import tpu as pltpu
from jax.sharding import PartitionSpec as P

C = 768
H = 16
HEAD = C // H
CA = 128
AH = 4
QW = 32
KW = 128
HALO = 48
NB = 2
EDGE = 16
REACH = EDGE + 64
TOKD = 32
ATOMD = 256
ROWS = 48
QROWS = 34 * H
KEYS = 1024
HALF = 512
CHUNK = 32
INFO = REACH + AH * EDGE
PACK = INFO + 16
F32 = jnp.float32
BF16 = jnp.bfloat16

NT = (((1,), (1,)), ((), ()))


def params(mib):
    return pltpu.CompilerParams(vmem_limit_bytes=mib * 1024 * 1024)


VMEM = pl.BlockSpec(memory_space=pltpu.VMEM)


def layer_norm(values):
    average = jnp.mean(values, axis=-1, keepdims=True)
    centred = values - average
    variance = jnp.mean(centred * centred, axis=-1, keepdims=True)
    return centred * lax.rsqrt(variance + 1e-05)


def tree(combine, parts):
    while len(parts) > 1:
        parts = [combine(*parts[i : i + 2]) if len(parts[i : i + 2]) == 2 else parts[i] for i in range(0, len(parts), 2)]
    return parts[0]


def along(reduce, values):
    return jnp.broadcast_to(reduce(values, axis=-1, keepdims=True), values.shape)


def chunk_starts(tok):
    core, y, x = lax.rem(tok, 2), lax.rem(tok // 2, 4), tok // 8
    starts = []
    for j in range(32):
        slow, fast = (j % 16) // 4, j % 4
        plane = core if j < 16 else 1 - core
        kx = jnp.where(plane == 0, slow, fast)
        ky = jnp.where(plane == 0, fast, slow)
        starts.append((((x ^ kx) * 4 + (y ^ ky)) * 2 + plane) * CHUNK)
    return starts


def ordered(pair_ref, t, starts):
    return jnp.concatenate(
        [pair_ref[t, pl.ds(pl.multiple_of(s, CHUNK), CHUNK), :] for s in starts], axis=0
    )


def for_neighbours(core, apart_ref, beside_ref, fill):
    for first, refs in ((0, (apart_ref, beside_ref)), (1, (beside_ref, apart_ref))):
        @pl.when(core == first)
        def _():
            for side, ref in enumerate(refs):
                fill(side, ref)


def pack_kernel(*refs):
    sources, targets, sems = refs[:6], refs[8:14], refs[14]
    apart_ref, beside_ref = refs[6:8]
    single_ref, edge_ref, token_ref = targets[:3]
    copies = [
        pltpu.make_async_copy(source, target, sems.at[i])
        for i, (source, target) in enumerate(zip(sources, targets))
    ]
    for copy in copies:
        copy.start()
    tok = lax.axis_index("tok")
    for copy in copies[:3]:
        copy.wait()

    def fill(side, out_ref):
        rows = slice(0, REACH) if side == 0 else slice(ATOMD - REACH, ATOMD)
        edge = slice(0, EDGE) if side == 0 else slice(ATOMD - EDGE, ATOMD)
        out_ref[:REACH] = single_ref[rows]
        for h in range(AH):
            out_ref[REACH + EDGE * h : REACH + EDGE * (h + 1)] = edge_ref[edge, h * KW : (h + 1) * KW]
        relative = (token_ref[:, side * 128 : (side + 1) * 128] - tok * TOKD).astype(F32)
        out_ref[INFO : INFO + 16] = jnp.broadcast_to(relative, (16, 128)).astype(BF16)

    for_neighbours(lax.rem(tok, 2), apart_ref, beside_ref, fill)
    for copy in copies[3:]:
        copy.wait()


def bias_kernel(pair_ref, pair_w_ref, bias0_ref, bias1_ref):
    starts = chunk_starts(lax.axis_index("tok"))
    weights = pair_w_ref[...]
    for t in range(TOKD):
        rows = ordered(pair_ref, t, starts)
        out = lax.dot_general(weights, rows, NT, preferred_element_type=F32).astype(BF16)
        bias0_ref[t * H : (t + 1) * H] = out[:H]
        bias1_ref[t * H : (t + 1) * H] = out[H:]


def windowed(proj_ref, windows, first_atom):
    head_of_lane = lax.broadcasted_iota(jnp.int32, (1, CA), 1) // (CA // AH)
    heads = [head_of_lane == h for h in range(AH)]
    lane = lax.broadcasted_iota(jnp.int32, (1, KW), 1)
    products = []
    for k_row, q_row, count, bias in windows:
        queries = proj_ref[q_row : q_row + count, :CA]
        stacked = jnp.concatenate([jnp.where(head, queries, jnp.zeros_like(queries)) for head in heads], axis=0)
        keys = proj_ref[k_row : k_row + KW, CA : 2 * CA]
        products.append(lax.dot_general(stacked, keys, NT, preferred_element_type=F32))
    scores = []
    for product, (k_row, q_row, count, bias) in zip(products, windows):
        position = first_atom + k_row + lane
        inside = (position >= 0) & (position < 32 * ATOMD)
        score = product * (CA // AH) ** (-0.5) + jnp.concatenate(bias, axis=0).astype(F32)
        scores.append(jnp.where(inside, score, -1000000000.0))
    scores = jnp.concatenate(scores, axis=0)
    powers = jnp.exp(scores - along(jnp.max, scores))
    share = 1.0 / along(jnp.sum, powers)
    weights = powers.astype(BF16)
    mixed = []
    first = 0
    for k_row, q_row, count, bias in windows:
        values = proj_ref[k_row : k_row + KW, 2 * CA :]
        rows = slice(first, first + AH * count)
        mixed.append(jnp.dot(weights[rows], values, preferred_element_type=F32) * share[rows])
        first += AH * count
    merged = []
    for rows, (k_row, q_row, count, bias) in zip(mixed, windows):
        out = jnp.where(heads[0], rows[:count], 0.0)
        for h in range(1, AH):
            out = jnp.where(heads[h], rows[h * count : (h + 1) * count], out)
        merged.append(out.astype(BF16))
    return merged


def projected(rows, qkv_ref):
    normed = layer_norm(rows.astype(F32)).astype(BF16)
    return jnp.dot(normed, qkv_ref[...], preferred_element_type=F32).astype(BF16)


def own_bias(bias_ref, w):
    return [bias_ref[QW * w : QW * (w + 1), h * KW : (h + 1) * KW] for h in range(AH)]


def wanted_tokens():
    row = lax.broadcasted_iota(jnp.int32, (ROWS, 1), 0)
    return jnp.where(row < TOKD, row, jnp.where(row == TOKD, -1, jnp.where(row == TOKD + 1, TOKD, -200)))


def hidden_and_sums(hidden_in, mixed, relative, out_w_ref, agg_ref):
    hidden = (
        hidden_in.astype(F32) + jnp.dot(mixed, out_w_ref[...], preferred_element_type=F32)
    ).astype(BF16)
    lifted = jnp.maximum(jnp.dot(hidden, agg_ref[...], preferred_element_type=F32), 0.0)
    member = (relative == wanted_tokens()).astype(F32)
    counts = jnp.sum(member, axis=-1, keepdims=True)
    picker = member.astype(BF16)
    upper = lifted.astype(BF16)
    lower = (lifted - upper.astype(F32)).astype(BF16)
    sums = jnp.dot(picker, upper, preferred_element_type=F32)
    sums = sums + jnp.dot(picker, lower, preferred_element_type=F32)
    return hidden, sums, counts


def inner_atom_kernel(single_ref, bias_ref, token_ref, qkv_ref, out_w_ref, agg_ref,
                      proj_ref, hidden_ref, sums_ref, counts_ref, pick_ref, mask_ref):
    tok = lax.axis_index("tok")
    proj_ref[...] = projected(single_ref[...], qkv_ref)
    windows = [(QW * w - HALO, QW * w, QW, own_bias(bias_ref, w)) for w in (4, 5, 2, 3)]
    mixed = jnp.concatenate(windowed(proj_ref, windows, tok * ATOMD), axis=0)
    lane = lax.broadcasted_iota(jnp.int32, (1, 128), 1)
    relative = jnp.where(lane < 64, token_ref[:, 128:], token_ref[:, :128]) - tok * TOKD
    hidden_in = jnp.concatenate([single_ref[128:192], single_ref[64:128]], axis=0)
    hidden, sums, counts = hidden_and_sums(hidden_in, mixed, relative, out_w_ref, agg_ref)
    hidden_ref[:64] = hidden[64:]
    hidden_ref[64:] = hidden[:64]
    sums_ref[...] = sums
    counts_ref[...] = jnp.broadcast_to(counts, counts_ref.shape)
    member = (token_ref[...] - tok * TOKD == wanted_tokens()).astype(F32)
    member = jnp.concatenate([member, jnp.zeros((128 - ROWS, ATOMD), F32)], axis=0)
    pick_ref[...] = member.T.astype(BF16)
    mask_ref[...] = head_mask().astype(F32).astype(BF16)


def atom_kernel(single_ref, apart_ref, beside_ref, bias_ref, token_ref, qkv_ref, out_w_ref, agg_ref,
                inner_ref, inner_hidden_ref, inner_sums_ref, inner_counts_ref,
                hidden_ref, stream_ref, normed_ref, own_ref, proj_ref, both_ref):
    tok = lax.axis_index("tok")
    core = lax.rem(tok, 2)
    both_ref[0] = apart_ref[...]
    both_ref[1] = beside_ref[...]
    lower_ref, upper_ref = both_ref.at[core], both_ref.at[1 - core]
    first_atom = tok * ATOMD - REACH
    beside = projected(jnp.concatenate([lower_ref[:REACH], upper_ref[:REACH]], axis=0), qkv_ref)
    proj_ref[:REACH] = beside[:REACH]
    proj_ref[REACH : REACH + ATOMD] = inner_ref[...]
    proj_ref[REACH + ATOMD :] = beside[REACH:]
    windows = [(32 + QW * w, REACH + QW * w, QW, own_bias(bias_ref, w)) for w in (0, 1, 6, 7)]
    for k_row, q_row, ref in ((288, REACH + ATOMD, upper_ref), (0, REACH - EDGE, lower_ref)):
        windows.append((k_row, q_row, EDGE, [ref[REACH + EDGE * h : REACH + EDGE * (h + 1)] for h in range(AH)]))
    mixed = windowed(proj_ref, windows, first_atom)
    mixed.insert(5, jnp.zeros((128 - 2 * EDGE, CA), BF16))
    hidden_in = jnp.concatenate(
        [
            single_ref[:64],
            single_ref[192:],
            upper_ref[:EDGE],
            jnp.zeros((128 - 2 * EDGE, CA), BF16),
            lower_ref[REACH - EDGE : REACH],
        ],
        axis=0,
    )
    lane = lax.broadcasted_iota(jnp.int32, (1, 128), 1)
    after = upper_ref[INFO : INFO + 16][:1].astype(F32).astype(jnp.int32) + TOKD
    before = lower_ref[INFO : INFO + 16][:1].astype(F32).astype(jnp.int32) - TOKD
    near = jnp.where(lane < EDGE, after, jnp.where(lane >= 128 - EDGE, before, -100))
    outer = jnp.where(lane < 64, token_ref[:, :128], token_ref[:, 128:]) - tok * TOKD
    hidden, sums, counts = hidden_and_sums(
        hidden_in, jnp.concatenate(mixed, axis=0), jnp.concatenate([outer, near], axis=1), out_w_ref, agg_ref
    )
    hidden_ref[:64] = hidden[:64]
    hidden_ref[64:192] = inner_hidden_ref[...]
    hidden_ref[192:] = hidden[64:128]
    stream = (sums + inner_sums_ref[...]) / jnp.maximum(counts + inner_counts_ref[:, :1], 1.0)
    stream_ref[...] = stream
    out = layer_norm(stream).astype(BF16)
    normed_ref[...] = out
    own_ref[...] = out[:TOKD]


def head_mask():
    row = lax.broadcasted_iota(jnp.int32, (QROWS, 1), 0)
    lane = lax.broadcasted_iota(jnp.int32, (1, C), 1)
    start = (row & (H - 1)) * HEAD
    return (lane >= start) & (lane < start + HEAD)


def query_kernel(layer, normed_ref, qkv_ref, out_ref):
    queries = jnp.dot(normed_ref[...], qkv_ref[layer, :, :C], preferred_element_type=F32).astype(BF16)
    row = lax.broadcasted_iota(jnp.int32, (QROWS, ROWS), 0)
    column = lax.broadcasted_iota(jnp.int32, (QROWS, ROWS), 1)
    spread = ((row >> 4) == column).astype(F32).astype(BF16)
    repeated = jnp.dot(spread, queries, preferred_element_type=F32)
    repeated = jnp.where(head_mask(), repeated, 0.0).astype(BF16)
    lifted = lax.dot_general(repeated, qkv_ref[layer, :, C : 2 * C], NT, preferred_element_type=F32)
    out_ref[...] = (lifted * HEAD ** (-0.5)).astype(BF16)


def first_query_kernel(normed_ref, qkv_ref, pair_hbm, pair_w_hbm, out_ref, apart_ref, beside_ref,
                       pair_ref, pair_w_ref, sems):
    copies = [
        pltpu.make_async_copy(pair_w_hbm, pair_w_ref, sems.at[0]),
        pltpu.make_async_copy(pair_hbm.at[0], pair_ref.at[0], sems.at[1]),
        pltpu.make_async_copy(pair_hbm.at[TOKD - 1], pair_ref.at[1], sems.at[2]),
    ]
    for copy in copies:
        copy.start()
    query_kernel(0, normed_ref, qkv_ref, out_ref)
    for copy in copies:
        copy.wait()
    tok = lax.axis_index("tok")
    outs = []
    for side, owner in enumerate((jnp.maximum(tok - 1, 0), jnp.minimum(tok + 1, 31))):
        rows = ordered(pair_ref, side, chunk_starts(owner))
        outs.append(lax.dot_general(pair_w_ref[...], rows, NT, preferred_element_type=F32).astype(BF16))

    def fill(side, ref):
        ref[...] = outs[side]

    for_neighbours(lax.rem(tok, 2), apart_ref, beside_ref, fill)


def join_edges_kernel(places, *refs):
    join_kernel(places, *refs[:3], refs[6])
    both_ref = refs[9]
    both_ref[0] = refs[3][...]
    both_ref[1] = refs[4][...]
    core = lax.rem(lax.axis_index("tok"), 2)
    for block, ref in enumerate(refs[7:9]):
        for side, index in enumerate((core, 1 - core)):
            ref[side * H : (side + 1) * H] = both_ref[index, block * H : (block + 1) * H]


def join_kernel(places, *refs):
    out_ref = refs[-1]
    rows = out_ref.shape[0] // len(places)
    for i, place in enumerate(places):
        out_ref[place * rows : (place + 1) * rows] = refs[i][...]


def scored(query_ref, rows, bias_ref, edge_bias_ref, half):
    scores = lax.dot_general(query_ref[...], rows, NT, preferred_element_type=F32)
    parts = []
    for k in range(HALF // 128):
        lanes = slice(half * HALF + 128 * k, half * HALF + 128 * (k + 1))
        bias = jnp.concatenate([bias_ref[:, lanes], edge_bias_ref[:, lanes]], axis=0)
        parts.append(scores[:, 128 * k : 128 * (k + 1)] + bias.astype(F32))
    return parts


def weighted(powers, rows):
    weights = jnp.concatenate([part.astype(BF16) for part in powers], axis=1)
    return jnp.dot(weights, rows, preferred_element_type=F32)


def near_kernel(query_ref, quad_ref, rest_ref, bias_ref, edge_bias_ref, mixed_ref, maximum_ref, total_ref):
    rows = jnp.concatenate([quad_ref[...], rest_ref[...]], axis=0)
    scores = scored(query_ref, rows, bias_ref, edge_bias_ref, 0)
    maximum = along(jnp.max, tree(jnp.maximum, scores))
    powers = [jnp.exp(part - maximum) for part in scores]
    maximum_ref[...] = maximum
    total_ref[...] = tree(jnp.add, powers)
    mixed_ref[...] = weighted(powers, rows)


def attend(layer, query_ref, quad_ref, rest_ref, bias_ref, edge_bias_ref, mixed_ref, maximum_ref, total_ref, mask_ref,
           qkv_ref, out_w_ref, stream_ref):
    rows = jnp.concatenate([quad_ref[...], rest_ref[...]], axis=0)
    scores = scored(query_ref, rows, bias_ref, edge_bias_ref, 1)
    maximum = jnp.maximum(maximum_ref[...], along(jnp.max, tree(jnp.maximum, scores)))
    powers = [jnp.exp(part - maximum) for part in scores]
    fade = jnp.exp(maximum_ref[...] - maximum)
    share = 1.0 / along(jnp.sum, total_ref[...] * fade + tree(jnp.add, powers))
    fade = fade * share
    new = weighted(powers, rows)
    mixed = jnp.concatenate(
        [
            (mixed_ref[:, 128 * k : 128 * (k + 1)] * fade + new[:, 128 * k : 128 * (k + 1)] * share).astype(BF16)
            for k in range(C // 128)
        ],
        axis=1,
    )
    valued = jnp.dot(mixed, qkv_ref[layer, :, 2 * C :], preferred_element_type=F32).astype(BF16) * mask_ref[...]
    row = lax.broadcasted_iota(jnp.int32, (ROWS, QROWS), 0)
    column = lax.broadcasted_iota(jnp.int32, (ROWS, QROWS), 1)
    gather = ((column >> 4) == row).astype(F32).astype(BF16)
    heads = jnp.dot(gather, valued, preferred_element_type=F32).astype(BF16)
    return stream_ref[...] + jnp.dot(heads, out_w_ref[layer], preferred_element_type=F32)


def middle_kernel(*refs):
    stream_ref, normed_ref, own_ref = refs[12:]
    stream = attend(0, *refs[:12])
    stream_ref[...] = stream
    out = layer_norm(stream).astype(BF16)
    normed_ref[...] = out
    own_ref[...] = out[:TOKD]


def last_kernel(*refs):
    bcast_ref, pick_ref, hidden_ref, atom_out_ref, token_out_ref = refs[12:]
    token_out = attend(1, *refs[:12]).astype(BF16)
    token_out_ref[...] = token_out[:TOKD]
    carry = jnp.dot(token_out, bcast_ref[...], preferred_element_type=F32).astype(BF16)
    picked = jnp.dot(pick_ref[:, :ROWS], carry, preferred_element_type=F32)
    atom_out_ref[...] = (hidden_ref[...].astype(F32) + picked).astype(BF16)


def flips(dx, dy, dc):
    pairs = []
    for tok in range(32):
        core, y, x = tok % 2, (tok // 2) % 4, tok // 8
        pairs.append((tok, ((x ^ dx) * 4 + (y ^ dy)) * 2 + (core ^ dc)))
    return pairs


def crossed(k, first):
    along_y, along_x = flips(0, k, 0), flips(k, 0, 0)
    return [
        (along_y if (tok % 2 == 0) == first else along_x)[tok] for tok in range(32)
    ]


def join(pieces, places, after=()):
    return pl.pallas_call(
        functools.partial(join_kernel, places),
        in_specs=[VMEM] * len(pieces) + [pl.BlockSpec(memory_space=pl.ANY)] * len(after),
        out_specs=VMEM,
        out_shape=shape(len(pieces) * pieces[0].shape[0], C),
        compiler_params=params(4),
        name="join",
    )(*pieces, *after)


ORDER = (2, 3, 1)


def exchange(rows, first):
    return [lax.ppermute(rows, "tok", crossed(k, first)) for k in ORDER]


def in_hbm(*arrays):
    return [pltpu.with_memory_space_constraint(x, pltpu.HBM) for x in arrays]


def shape(rows, columns, dtype=BF16):
    return jax.ShapeDtypeStruct((rows, columns), dtype)


def local(atom_single, atom_bias, atom_token, atom_counts, pair_rep, atom_qkv_w, atom_out_w, agg_w,
          tok_qkv_w, tok_out_w, pair_w, bcast_w):
    tokens = atom_token.reshape(1, ATOMD)
    pair_wt = pair_w.T
    hbm = pl.BlockSpec(memory_space=pltpu.HBM)

    small = (atom_single, atom_bias, tokens, atom_qkv_w, atom_out_w, agg_w)
    to_apart, to_beside, *small = pl.pallas_call(
        pack_kernel,
        in_specs=[hbm] * 6,
        out_specs=[VMEM] * 8,
        out_shape=[shape(PACK, CA)] * 2 + [jax.ShapeDtypeStruct(x.shape, x.dtype) for x in small],
        scratch_shapes=[pltpu.SemaphoreType.DMA((6,))],
        compiler_params=params(8),
        cost_estimate=pl.CostEstimate(flops=4 * 10**9, bytes_accessed=16 * 2**20, transcendentals=0),
        name="pack",
    )(*in_hbm(*small))
    across = [(i, (i + (1 if i % 2 else -1)) % 32) for i in range(32)]
    apart = lax.ppermute(to_apart, "tok", across)
    beside = lax.ppermute(to_beside, "tok", flips(0, 0, 1))

    bias = pl.pallas_call(
        bias_kernel,
        in_specs=[VMEM] * 2,
        out_specs=[VMEM] * 2,
        out_shape=[shape(TOKD * H, KEYS)] * 2,
        compiler_params=params(12),
        cost_estimate=pl.CostEstimate(flops=2 * 32 * 1024 * 128 * 32, bytes_accessed=10 * 2**20, transcendentals=0),
        name="bias",
    )(pair_rep, pair_wt)

    *inner, pick, mask = pl.pallas_call(
        inner_atom_kernel,
        in_specs=[VMEM] * 6,
        out_specs=[VMEM] * 6,
        out_shape=[
            shape(ATOMD, 3 * CA),
            shape(4 * QW, CA),
            shape(ROWS, C, F32),
            shape(ROWS, 128, F32),
            shape(ATOMD, 128),
            shape(QROWS, C),
        ],
        compiler_params=params(8),
        cost_estimate=pl.CostEstimate(flops=4 * 10**9, bytes_accessed=16 * 2**20, transcendentals=0),
        name="inner_atoms",
    )(*small)
    hidden, stream, normed, own = pl.pallas_call(
        atom_kernel,
        in_specs=[VMEM] * 12,
        out_specs=[VMEM] * 4,
        out_shape=[shape(ATOMD, CA), shape(ROWS, C, F32), shape(ROWS, C), shape(TOKD, C)],
        scratch_shapes=[pltpu.VMEM((2 * REACH + ATOMD, 3 * CA), BF16), pltpu.VMEM((2, PACK, CA), BF16)],
        compiler_params=params(8),
        cost_estimate=pl.CostEstimate(flops=4 * 10**9, bytes_accessed=16 * 2**20, transcendentals=0),
        name="atoms",
    )(small[0], apart, beside, *small[1:], *inner)

    for layer in range(2):
        pieces = [own] + exchange(own, True)
        if layer == 0:
            queries, *edges = pl.pallas_call(
                first_query_kernel,
                in_specs=[VMEM] * 2 + [hbm] * 2,
                out_specs=[VMEM] * 3,
                out_shape=[shape(QROWS, C)] + [shape(NB * H, KEYS)] * 2,
                scratch_shapes=[
                    pltpu.VMEM((2, KEYS, 128), BF16),
                    pltpu.VMEM((32, 128), BF16),
                    pltpu.SemaphoreType.DMA((3,)),
                ],
                compiler_params=params(16),
                cost_estimate=pl.CostEstimate(flops=10**9, bytes_accessed=5 * 2**20, transcendentals=0),
                name="queries",
            )(normed, tok_qkv_w, *in_hbm(pair_rep, pair_wt))
            edges = [lax.ppermute(edges[0], "tok", across), lax.ppermute(edges[1], "tok", flips(0, 0, 1))]
        else:
            queries = pl.pallas_call(
                functools.partial(query_kernel, layer),
                in_specs=[VMEM] * 2,
                out_specs=VMEM,
                out_shape=shape(QROWS, C),
                compiler_params=params(16),
                cost_estimate=pl.CostEstimate(flops=10**9, bytes_accessed=5 * 2**20, transcendentals=0),
                name="queries",
            )(normed, tok_qkv_w)
        quad = join(pieces, (0, *ORDER), [queries])
        far_quad = lax.ppermute(quad, "tok", flips(0, 0, 1))
        pieces = exchange(quad, False)
        places = tuple(k - 1 for k in ORDER)
        if layer == 0:
            rest, *edge_bias = pl.pallas_call(
                functools.partial(join_edges_kernel, places),
                in_specs=[VMEM] * 5 + [pl.BlockSpec(memory_space=pl.ANY)],
                out_specs=[VMEM] * 3,
                out_shape=[shape(HALF * 3 // 4, C)] + [shape(2 * H, KEYS)] * 2,
                scratch_shapes=[pltpu.VMEM((2, NB * H, KEYS), BF16)],
                compiler_params=params(8),
                name="join",
            )(*pieces, *edges, bias[0])
        else:
            rest = join(pieces, places, [far_quad])
        far_rest = lax.ppermute(rest, "tok", flips(0, 0, 1))
        partial = pl.pallas_call(
            near_kernel,
            in_specs=[VMEM] * 5,
            out_specs=[VMEM] * 3,
            out_shape=[shape(QROWS, C, F32)] + [shape(QROWS, 128, F32)] * 2,
            compiler_params=params(16),
            cost_estimate=pl.CostEstimate(flops=2 * 10**9, bytes_accessed=5 * 2**20, transcendentals=300000),
            name="near",
        )(queries, quad, rest, bias[layer], edge_bias[layer])
        operands = (queries, far_quad, far_rest, bias[layer], edge_bias[layer], *partial, mask, tok_qkv_w, tok_out_w, stream)
        if layer == 0:
            stream, normed, own = pl.pallas_call(
                middle_kernel,
                in_specs=[VMEM] * 12,
                out_specs=[VMEM] * 3,
                out_shape=[shape(ROWS, C, F32), shape(ROWS, C), shape(TOKD, C)],
                compiler_params=params(16),
                name="block",
            )(*operands)
        else:
            atom_out, token_out = pl.pallas_call(
                last_kernel,
                in_specs=[VMEM] * 15,
                out_specs=[VMEM] * 2,
                out_shape=[shape(ATOMD, CA), shape(TOKD, C)],
                compiler_params=params(16),
                name="block_and_broadcast",
            )(*operands, bcast_w, pick, hidden)
    return (atom_out, token_out)


def solution(mesh):
    placed = (
        P(("seed", "tok"), None),
        P("tok", None),
        P("tok"),
        P("tok"),
        P("tok", None, None),
        P(),
        P(),
        P(),
        P(),
        P(),
        P(),
        P(),
    )
    return jax.shard_map(
        local,
        mesh=mesh,
        in_specs=placed,
        out_specs=(P(("seed", "tok"), None), P(("seed", "tok"), None)),
        check_vma=False,
    )
```

```python
import functools

import jax
import jax.numpy as jnp
from jax import lax
from jax.experimental import pallas as pl
from jax.experimental.pallas import tpu as pltpu
from jax.sharding import PartitionSpec as P

C = 768
H = 16
HEAD = C // H
CA = 128
AH = 4
QW = 32
KW = 128
HALO = 48
NB = 2
EDGE = 16
REACH = EDGE + 64
TOKD = 32
ATOMD = 256
ROWS = 48
QROWS = 34 * H
KEYS = 1024
HALF = 512
CHUNK = 32
INFO = REACH + AH * EDGE
PACK = INFO + 16
F32 = jnp.float32
BF16 = jnp.bfloat16

NT = (((1,), (1,)), ((), ()))


def params(mib):
    return pltpu.CompilerParams(vmem_limit_bytes=mib * 1024 * 1024)


VMEM = pl.BlockSpec(memory_space=pltpu.VMEM)


def layer_norm(values):
    average = jnp.mean(values, axis=-1, keepdims=True)
    centred = values - average
    variance = jnp.mean(centred * centred, axis=-1, keepdims=True)
    return centred * lax.rsqrt(variance + 1e-05)


def tree(combine, parts):
    while len(parts) > 1:
        parts = [combine(*parts[i : i + 2]) if len(parts[i : i + 2]) == 2 else parts[i] for i in range(0, len(parts), 2)]
    return parts[0]


def along(reduce, values):
    return jnp.broadcast_to(reduce(values, axis=-1, keepdims=True), values.shape)


def chunk_starts(tok):
    core, y, x = lax.rem(tok, 2), lax.rem(tok // 2, 4), tok // 8
    starts = []
    for j in range(32):
        slow, fast = (j % 16) // 4, j % 4
        plane = core if j < 16 else 1 - core
        kx = jnp.where(plane == 0, slow, fast)
        ky = jnp.where(plane == 0, fast, slow)
        starts.append((((x ^ kx) * 4 + (y ^ ky)) * 2 + plane) * CHUNK)
    return starts


def ordered(pair_ref, t, starts):
    return jnp.concatenate(
        [pair_ref[t, pl.ds(pl.multiple_of(s, CHUNK), CHUNK), :] for s in starts], axis=0
    )


def for_neighbours(core, apart_ref, beside_ref, fill):
    for first, refs in ((0, (apart_ref, beside_ref)), (1, (beside_ref, apart_ref))):
        @pl.when(core == first)
        def _():
            for side, ref in enumerate(refs):
                fill(side, ref)


def pack_kernel(*refs):
    sources, targets, sems = refs[:6], refs[8:14], refs[14]
    apart_ref, beside_ref = refs[6:8]
    single_ref, edge_ref, token_ref = targets[:3]
    copies = [
        pltpu.make_async_copy(source, target, sems.at[i])
        for i, (source, target) in enumerate(zip(sources, targets))
    ]
    for copy in copies:
        copy.start()
    tok = lax.axis_index("tok")
    for copy in copies[:3]:
        copy.wait()

    def fill(side, out_ref):
        rows = slice(0, REACH) if side == 0 else slice(ATOMD - REACH, ATOMD)
        edge = slice(0, EDGE) if side == 0 else slice(ATOMD - EDGE, ATOMD)
        out_ref[:REACH] = single_ref[rows]
        for h in range(AH):
            out_ref[REACH + EDGE * h : REACH + EDGE * (h + 1)] = edge_ref[edge, h * KW : (h + 1) * KW]
        relative = (token_ref[:, side * 128 : (side + 1) * 128] - tok * TOKD).astype(F32)
        out_ref[INFO : INFO + 16] = jnp.broadcast_to(relative, (16, 128)).astype(BF16)

    for_neighbours(lax.rem(tok, 2), apart_ref, beside_ref, fill)
    for copy in copies[3:]:
        copy.wait()


def bias_kernel(pair_ref, pair_w_ref, bias0_ref, bias1_ref):
    starts = chunk_starts(lax.axis_index("tok"))
    weights = pair_w_ref[...]
    for t in range(TOKD):
        rows = ordered(pair_ref, t, starts)
        out = lax.dot_general(weights, rows, NT, preferred_element_type=F32).astype(BF16)
        bias0_ref[t * H : (t + 1) * H] = out[:H]
        bias1_ref[t * H : (t + 1) * H] = out[H:]


def windowed(proj_ref, windows, first_atom):
    head_of_lane = lax.broadcasted_iota(jnp.int32, (1, CA), 1) // (CA // AH)
    heads = [head_of_lane == h for h in range(AH)]
    lane = lax.broadcasted_iota(jnp.int32, (1, KW), 1)
    products = []
    for k_row, q_row, count, bias in windows:
        queries = proj_ref[q_row : q_row + count, :CA]
        stacked = jnp.concatenate([jnp.where(head, queries, jnp.zeros_like(queries)) for head in heads], axis=0)
        keys = proj_ref[k_row : k_row + KW, CA : 2 * CA]
        products.append(lax.dot_general(stacked, keys, NT, preferred_element_type=F32))
    scores = []
    for product, (k_row, q_row, count, bias) in zip(products, windows):
        position = first_atom + k_row + lane
        inside = (position >= 0) & (position < 32 * ATOMD)
        score = product * (CA // AH) ** (-0.5) + jnp.concatenate(bias, axis=0).astype(F32)
        scores.append(jnp.where(inside, score, -1000000000.0))
    scores = jnp.concatenate(scores, axis=0)
    powers = jnp.exp(scores - along(jnp.max, scores))
    share = 1.0 / along(jnp.sum, powers)
    weights = powers.astype(BF16)
    mixed = []
    first = 0
    for k_row, q_row, count, bias in windows:
        values = proj_ref[k_row : k_row + KW, 2 * CA :]
        rows = slice(first, first + AH * count)
        mixed.append(jnp.dot(weights[rows], values, preferred_element_type=F32) * share[rows])
        first += AH * count
    merged = []
    for rows, (k_row, q_row, count, bias) in zip(mixed, windows):
        out = jnp.where(heads[0], rows[:count], 0.0)
        for h in range(1, AH):
            out = jnp.where(heads[h], rows[h * count : (h + 1) * count], out)
        merged.append(out.astype(BF16))
    return merged


def projected(rows, qkv_ref):
    normed = layer_norm(rows.astype(F32)).astype(BF16)
    return jnp.dot(normed, qkv_ref[...], preferred_element_type=F32).astype(BF16)


def own_bias(bias_ref, w):
    return [bias_ref[QW * w : QW * (w + 1), h * KW : (h + 1) * KW] for h in range(AH)]


def wanted_tokens():
    row = lax.broadcasted_iota(jnp.int32, (ROWS, 1), 0)
    return jnp.where(row < TOKD, row, jnp.where(row == TOKD, -1, jnp.where(row == TOKD + 1, TOKD, -200)))


def hidden_and_sums(hidden_in, mixed, relative, out_w_ref, agg_ref):
    hidden = (
        hidden_in.astype(F32) + jnp.dot(mixed, out_w_ref[...], preferred_element_type=F32)
    ).astype(BF16)
    lifted = jnp.maximum(jnp.dot(hidden, agg_ref[...], preferred_element_type=F32), 0.0)
    member = (relative == wanted_tokens()).astype(F32)
    counts = jnp.sum(member, axis=-1, keepdims=True)
    picker = member.astype(BF16)
    upper = lifted.astype(BF16)
    lower = (lifted - upper.astype(F32)).astype(BF16)
    sums = jnp.dot(picker, upper, preferred_element_type=F32)
    sums = sums + jnp.dot(picker, lower, preferred_element_type=F32)
    return hidden, sums, counts


def inner_atom_kernel(single_ref, bias_ref, token_ref, qkv_ref, out_w_ref, agg_ref,
                      proj_ref, hidden_ref, sums_ref, counts_ref, pick_ref):
    tok = lax.axis_index("tok")
    proj_ref[...] = projected(single_ref[...], qkv_ref)
    windows = [(QW * w - HALO, QW * w, QW, own_bias(bias_ref, w)) for w in (4, 5, 2, 3)]
    mixed = jnp.concatenate(windowed(proj_ref, windows, tok * ATOMD), axis=0)
    lane = lax.broadcasted_iota(jnp.int32, (1, 128), 1)
    relative = jnp.where(lane < 64, token_ref[:, 128:], token_ref[:, :128]) - tok * TOKD
    hidden_in = jnp.concatenate([single_ref[128:192], single_ref[64:128]], axis=0)
    hidden, sums, counts = hidden_and_sums(hidden_in, mixed, relative, out_w_ref, agg_ref)
    hidden_ref[:64] = hidden[64:]
    hidden_ref[64:] = hidden[:64]
    sums_ref[...] = sums
    counts_ref[...] = jnp.broadcast_to(counts, counts_ref.shape)
    member = (token_ref[...] - tok * TOKD == wanted_tokens()).astype(F32)
    member = jnp.concatenate([member, jnp.zeros((128 - ROWS, ATOMD), F32)], axis=0)
    pick_ref[...] = member.T.astype(BF16)


def atom_kernel(single_ref, apart_ref, beside_ref, bias_ref, token_ref, qkv_ref, out_w_ref, agg_ref,
                inner_ref, inner_hidden_ref, inner_sums_ref, inner_counts_ref,
                hidden_ref, stream_ref, normed_ref, own_ref, proj_ref, both_ref):
    tok = lax.axis_index("tok")
    core = lax.rem(tok, 2)
    both_ref[0] = apart_ref[...]
    both_ref[1] = beside_ref[...]
    lower_ref, upper_ref = both_ref.at[core], both_ref.at[1 - core]
    first_atom = tok * ATOMD - REACH
    beside = projected(jnp.concatenate([lower_ref[:REACH], upper_ref[:REACH]], axis=0), qkv_ref)
    proj_ref[:REACH] = beside[:REACH]
    proj_ref[REACH : REACH + ATOMD] = inner_ref[...]
    proj_ref[REACH + ATOMD :] = beside[REACH:]
    windows = [(32 + QW * w, REACH + QW * w, QW, own_bias(bias_ref, w)) for w in (0, 1, 6, 7)]
    for k_row, q_row, ref in ((288, REACH + ATOMD, upper_ref), (0, REACH - EDGE, lower_ref)):
        windows.append((k_row, q_row, EDGE, [ref[REACH + EDGE * h : REACH + EDGE * (h + 1)] for h in range(AH)]))
    mixed = windowed(proj_ref, windows, first_atom)
    mixed.insert(5, jnp.zeros((128 - 2 * EDGE, CA), BF16))
    hidden_in = jnp.concatenate(
        [
            single_ref[:64],
            single_ref[192:],
            upper_ref[:EDGE],
            jnp.zeros((128 - 2 * EDGE, CA), BF16),
            lower_ref[REACH - EDGE : REACH],
        ],
        axis=0,
    )
    lane = lax.broadcasted_iota(jnp.int32, (1, 128), 1)
    after = upper_ref[INFO : INFO + 16][:1].astype(F32).astype(jnp.int32) + TOKD
    before = lower_ref[INFO : INFO + 16][:1].astype(F32).astype(jnp.int32) - TOKD
    near = jnp.where(lane < EDGE, after, jnp.where(lane >= 128 - EDGE, before, -100))
    outer = jnp.where(lane < 64, token_ref[:, :128], token_ref[:, 128:]) - tok * TOKD
    hidden, sums, counts = hidden_and_sums(
        hidden_in, jnp.concatenate(mixed, axis=0), jnp.concatenate([outer, near], axis=1), out_w_ref, agg_ref
    )
    hidden_ref[:64] = hidden[:64]
    hidden_ref[64:192] = inner_hidden_ref[...]
    hidden_ref[192:] = hidden[64:128]
    stream = (sums + inner_sums_ref[...]) / jnp.maximum(counts + inner_counts_ref[:, :1], 1.0)
    stream_ref[...] = stream
    out = layer_norm(stream).astype(BF16)
    normed_ref[...] = out
    own_ref[...] = out[:TOKD]


def head_mask():
    row = lax.broadcasted_iota(jnp.int32, (QROWS, 1), 0)
    lane = lax.broadcasted_iota(jnp.int32, (1, C), 1)
    start = (row & (H - 1)) * HEAD
    return (lane >= start) & (lane < start + HEAD)


def query_kernel(layer, normed_ref, qkv_ref, out_ref):
    queries = jnp.dot(normed_ref[...], qkv_ref[layer, :, :C], preferred_element_type=F32).astype(BF16)
    row = lax.broadcasted_iota(jnp.int32, (QROWS, ROWS), 0)
    column = lax.broadcasted_iota(jnp.int32, (QROWS, ROWS), 1)
    spread = ((row >> 4) == column).astype(F32).astype(BF16)
    repeated = jnp.dot(spread, queries, preferred_element_type=F32)
    repeated = jnp.where(head_mask(), repeated, 0.0).astype(BF16)
    lifted = lax.dot_general(repeated, qkv_ref[layer, :, C : 2 * C], NT, preferred_element_type=F32)
    out_ref[...] = (lifted * HEAD ** (-0.5)).astype(BF16)


def first_query_kernel(normed_ref, qkv_ref, pair_hbm, pair_w_hbm, out_ref, apart_ref, beside_ref,
                       pair_ref, pair_w_ref, sems):
    copies = [
        pltpu.make_async_copy(pair_w_hbm, pair_w_ref, sems.at[0]),
        pltpu.make_async_copy(pair_hbm.at[0], pair_ref.at[0], sems.at[1]),
        pltpu.make_async_copy(pair_hbm.at[TOKD - 1], pair_ref.at[1], sems.at[2]),
    ]
    for copy in copies:
        copy.start()
    query_kernel(0, normed_ref, qkv_ref, out_ref)
    for copy in copies:
        copy.wait()
    tok = lax.axis_index("tok")
    outs = []
    for side, owner in enumerate((jnp.maximum(tok - 1, 0), jnp.minimum(tok + 1, 31))):
        rows = ordered(pair_ref, side, chunk_starts(owner))
        outs.append(lax.dot_general(pair_w_ref[...], rows, NT, preferred_element_type=F32).astype(BF16))

    def fill(side, ref):
        ref[...] = outs[side]

    for_neighbours(lax.rem(tok, 2), apart_ref, beside_ref, fill)


def join_edges_kernel(places, *refs):
    join_kernel(places, *refs[:3], refs[6])
    both_ref = refs[9]
    both_ref[0] = refs[3][...]
    both_ref[1] = refs[4][...]
    core = lax.rem(lax.axis_index("tok"), 2)
    for block, ref in enumerate(refs[7:9]):
        for side, index in enumerate((core, 1 - core)):
            ref[side * H : (side + 1) * H] = both_ref[index, block * H : (block + 1) * H]


def join_kernel(places, *refs):
    out_ref = refs[-1]
    rows = out_ref.shape[0] // len(places)
    for i, place in enumerate(places):
        out_ref[place * rows : (place + 1) * rows] = refs[i][...]


def scored(query_ref, rows, bias_ref, edge_bias_ref, half):
    scores = lax.dot_general(query_ref[...], rows, NT, preferred_element_type=F32)
    parts = []
    for k in range(HALF // 128):
        lanes = slice(half * HALF + 128 * k, half * HALF + 128 * (k + 1))
        bias = jnp.concatenate([bias_ref[:, lanes], edge_bias_ref[:, lanes]], axis=0)
        parts.append(scores[:, 128 * k : 128 * (k + 1)] + bias.astype(F32))
    return parts


def weighted(powers, rows):
    weights = jnp.concatenate([part.astype(BF16) for part in powers], axis=1)
    return jnp.dot(weights, rows, preferred_element_type=F32)


def near_kernel(query_ref, quad_ref, rest_ref, bias_ref, edge_bias_ref, mixed_ref, maximum_ref, total_ref, *mask_ref):
    for ref in mask_ref:
        ref[...] = head_mask().astype(F32).astype(BF16)
    rows = jnp.concatenate([quad_ref[...], rest_ref[...]], axis=0)
    scores = scored(query_ref, rows, bias_ref, edge_bias_ref, 0)
    maximum = along(jnp.max, tree(jnp.maximum, scores))
    powers = [jnp.exp(part - maximum) for part in scores]
    maximum_ref[...] = maximum
    total_ref[...] = tree(jnp.add, powers)
    mixed_ref[...] = weighted(powers, rows)


def attend(layer, query_ref, quad_ref, rest_ref, bias_ref, edge_bias_ref, mixed_ref, maximum_ref, total_ref, mask_ref,
           qkv_ref, out_w_ref, stream_ref):
    rows = jnp.concatenate([quad_ref[...], rest_ref[...]], axis=0)
    scores = scored(query_ref, rows, bias_ref, edge_bias_ref, 1)
    maximum = jnp.maximum(maximum_ref[...], along(jnp.max, tree(jnp.maximum, scores)))
    powers = [jnp.exp(part - maximum) for part in scores]
    fade = jnp.exp(maximum_ref[...] - maximum)
    share = 1.0 / along(jnp.sum, total_ref[...] * fade + tree(jnp.add, powers))
    fade = fade * share
    new = weighted(powers, rows)
    mixed = jnp.concatenate(
        [
            (mixed_ref[:, 128 * k : 128 * (k + 1)] * fade + new[:, 128 * k : 128 * (k + 1)] * share).astype(BF16)
            for k in range(C // 128)
        ],
        axis=1,
    )
    valued = jnp.dot(mixed, qkv_ref[layer, :, 2 * C :], preferred_element_type=F32).astype(BF16) * mask_ref[...]
    row = lax.broadcasted_iota(jnp.int32, (ROWS, QROWS), 0)
    column = lax.broadcasted_iota(jnp.int32, (ROWS, QROWS), 1)
    gather = ((column >> 4) == row).astype(F32).astype(BF16)
    heads = jnp.dot(gather, valued, preferred_element_type=F32).astype(BF16)
    return stream_ref[...] + jnp.dot(heads, out_w_ref[layer], preferred_element_type=F32)


def middle_kernel(*refs):
    stream_ref, normed_ref, own_ref = refs[12:]
    stream = attend(0, *refs[:12])
    stream_ref[...] = stream
    out = layer_norm(stream).astype(BF16)
    normed_ref[...] = out
    own_ref[...] = out[:TOKD]


def last_kernel(*refs):
    bcast_ref, pick_ref, hidden_ref, atom_out_ref, token_out_ref = refs[12:]
    token_out = attend(1, *refs[:12]).astype(BF16)
    token_out_ref[...] = token_out[:TOKD]
    carry = jnp.dot(token_out, bcast_ref[...], preferred_element_type=F32).astype(BF16)
    picked = jnp.dot(pick_ref[:, :ROWS], carry, preferred_element_type=F32)
    atom_out_ref[...] = (hidden_ref[...].astype(F32) + picked).astype(BF16)


def flips(dx, dy, dc):
    pairs = []
    for tok in range(32):
        core, y, x = tok % 2, (tok // 2) % 4, tok // 8
        pairs.append((tok, ((x ^ dx) * 4 + (y ^ dy)) * 2 + (core ^ dc)))
    return pairs


def crossed(k, first):
    along_y, along_x = flips(0, k, 0), flips(k, 0, 0)
    return [
        (along_y if (tok % 2 == 0) == first else along_x)[tok] for tok in range(32)
    ]


def join(pieces, places, after=()):
    return pl.pallas_call(
        functools.partial(join_kernel, places),
        in_specs=[VMEM] * len(pieces) + [pl.BlockSpec(memory_space=pl.ANY)] * len(after),
        out_specs=VMEM,
        out_shape=shape(len(pieces) * pieces[0].shape[0], C),
        compiler_params=params(4),
        name="join",
    )(*pieces, *after)


ORDER = (2, 3, 1)


def exchange(rows, first):
    return [lax.ppermute(rows, "tok", crossed(k, first)) for k in ORDER]


def in_hbm(*arrays):
    return [pltpu.with_memory_space_constraint(x, pltpu.HBM) for x in arrays]


def shape(rows, columns, dtype=BF16):
    return jax.ShapeDtypeStruct((rows, columns), dtype)


def local(atom_single, atom_bias, atom_token, atom_counts, pair_rep, atom_qkv_w, atom_out_w, agg_w,
          tok_qkv_w, tok_out_w, pair_w, bcast_w):
    tokens = atom_token.reshape(1, ATOMD)
    pair_wt = pair_w.T
    hbm = pl.BlockSpec(memory_space=pltpu.HBM)

    small = (atom_single, atom_bias, tokens, atom_qkv_w, atom_out_w, agg_w)
    to_apart, to_beside, *small = pl.pallas_call(
        pack_kernel,
        in_specs=[hbm] * 6,
        out_specs=[VMEM] * 8,
        out_shape=[shape(PACK, CA)] * 2 + [jax.ShapeDtypeStruct(x.shape, x.dtype) for x in small],
        scratch_shapes=[pltpu.SemaphoreType.DMA((6,))],
        compiler_params=params(8),
        cost_estimate=pl.CostEstimate(flops=4 * 10**9, bytes_accessed=16 * 2**20, transcendentals=0),
        name="pack",
    )(*in_hbm(*small))
    across = [(i, (i + (1 if i % 2 else -1)) % 32) for i in range(32)]
    apart = lax.ppermute(to_apart, "tok", across)
    beside = lax.ppermute(to_beside, "tok", flips(0, 0, 1))

    bias = pl.pallas_call(
        bias_kernel,
        in_specs=[VMEM] * 2,
        out_specs=[VMEM] * 2,
        out_shape=[shape(TOKD * H, KEYS)] * 2,
        compiler_params=params(12),
        cost_estimate=pl.CostEstimate(flops=2 * 32 * 1024 * 128 * 32, bytes_accessed=10 * 2**20, transcendentals=0),
        name="bias",
    )(pair_rep, pair_wt)

    *inner, pick = pl.pallas_call(
        inner_atom_kernel,
        in_specs=[VMEM] * 6,
        out_specs=[VMEM] * 5,
        out_shape=[
            shape(ATOMD, 3 * CA),
            shape(4 * QW, CA),
            shape(ROWS, C, F32),
            shape(ROWS, 128, F32),
            shape(ATOMD, 128),
        ],
        compiler_params=params(8),
        cost_estimate=pl.CostEstimate(flops=4 * 10**9, bytes_accessed=16 * 2**20, transcendentals=0),
        name="inner_atoms",
    )(*small)
    hidden, stream, normed, own = pl.pallas_call(
        atom_kernel,
        in_specs=[VMEM] * 12,
        out_specs=[VMEM] * 4,
        out_shape=[shape(ATOMD, CA), shape(ROWS, C, F32), shape(ROWS, C), shape(TOKD, C)],
        scratch_shapes=[pltpu.VMEM((2 * REACH + ATOMD, 3 * CA), BF16), pltpu.VMEM((2, PACK, CA), BF16)],
        compiler_params=params(8),
        cost_estimate=pl.CostEstimate(flops=4 * 10**9, bytes_accessed=16 * 2**20, transcendentals=0),
        name="atoms",
    )(small[0], apart, beside, *small[1:], *inner)

    for layer in range(2):
        pieces = [own] + exchange(own, True)
        if layer == 0:
            queries, *edges = pl.pallas_call(
                first_query_kernel,
                in_specs=[VMEM] * 2 + [hbm] * 2,
                out_specs=[VMEM] * 3,
                out_shape=[shape(QROWS, C)] + [shape(NB * H, KEYS)] * 2,
                scratch_shapes=[
                    pltpu.VMEM((2, KEYS, 128), BF16),
                    pltpu.VMEM((32, 128), BF16),
                    pltpu.SemaphoreType.DMA((3,)),
                ],
                compiler_params=params(16),
                cost_estimate=pl.CostEstimate(flops=10**9, bytes_accessed=5 * 2**20, transcendentals=0),
                name="queries",
            )(normed, tok_qkv_w, *in_hbm(pair_rep, pair_wt))
            edges = [lax.ppermute(edges[0], "tok", across), lax.ppermute(edges[1], "tok", flips(0, 0, 1))]
        else:
            queries = pl.pallas_call(
                functools.partial(query_kernel, layer),
                in_specs=[VMEM] * 2,
                out_specs=VMEM,
                out_shape=shape(QROWS, C),
                compiler_params=params(16),
                cost_estimate=pl.CostEstimate(flops=10**9, bytes_accessed=5 * 2**20, transcendentals=0),
                name="queries",
            )(normed, tok_qkv_w)
        quad = join(pieces, (0, *ORDER), [queries])
        far_quad = lax.ppermute(quad, "tok", flips(0, 0, 1))
        pieces = exchange(quad, False)
        places = tuple(k - 1 for k in ORDER)
        if layer == 0:
            rest, *edge_bias = pl.pallas_call(
                functools.partial(join_edges_kernel, places),
                in_specs=[VMEM] * 5 + [pl.BlockSpec(memory_space=pl.ANY)],
                out_specs=[VMEM] * 3,
                out_shape=[shape(HALF * 3 // 4, C)] + [shape(2 * H, KEYS)] * 2,
                scratch_shapes=[pltpu.VMEM((2, NB * H, KEYS), BF16)],
                compiler_params=params(8),
                name="join",
            )(*pieces, *edges, bias[0])
        else:
            rest = join(pieces, places, [far_quad])
        far_rest = lax.ppermute(rest, "tok", flips(0, 0, 1))
        made = pl.pallas_call(
            near_kernel,
            in_specs=[VMEM] * 5,
            out_specs=[VMEM] * (4 - layer),
            out_shape=[shape(QROWS, C, F32)] + [shape(QROWS, 128, F32)] * 2 + [shape(QROWS, C)] * (1 - layer),
            compiler_params=params(16),
            cost_estimate=pl.CostEstimate(flops=2 * 10**9, bytes_accessed=5 * 2**20, transcendentals=300000),
            name="near",
        )(queries, quad, rest, bias[layer], edge_bias[layer])
        partial = made[:3]
        mask = mask if layer else made[3]
        operands = (queries, far_quad, far_rest, bias[layer], edge_bias[layer], *partial, mask, tok_qkv_w, tok_out_w, stream)
        if layer == 0:
            stream, normed, own = pl.pallas_call(
                middle_kernel,
                in_specs=[VMEM] * 12,
                out_specs=[VMEM] * 3,
                out_shape=[shape(ROWS, C, F32), shape(ROWS, C), shape(TOKD, C)],
                compiler_params=params(16),
                name="block",
            )(*operands)
        else:
            atom_out, token_out = pl.pallas_call(
                last_kernel,
                in_specs=[VMEM] * 15,
                out_specs=[VMEM] * 2,
                out_shape=[shape(ATOMD, CA), shape(TOKD, C)],
                compiler_params=params(16),
                name="block_and_broadcast",
            )(*operands, bcast_w, pick, hidden)
    return (atom_out, token_out)


def solution(mesh):
    placed = (
        P(("seed", "tok"), None),
        P("tok", None),
        P("tok"),
        P("tok"),
        P("tok", None, None),
        P(),
        P(),
        P(),
        P(),
        P(),
        P(),
        P(),
    )
    return jax.shard_map(
        local,
        mesh=mesh,
        in_specs=placed,
        out_specs=(P(("seed", "tok"), None), P(("seed", "tok"), None)),
        check_vma=False,
    )
```
